128 devices in a mesh: group: 8 (over x_lo, y), tensor: 16 (over x_hi, z, core).
Axes of the slice: x: 4 (x_hi: 2, x_lo: 2; x = x_hi * 2 + x_lo), y: 4, z: 4, core: 2. Of those that a mesh axis runs over, the one named last changes fastest.
Arguments:
- backbone_hidden: bfloat16 [1024, 27648], P('group', 'tensor'), may hold values from -6 to 6
- backbone_down: bfloat16 [27648, 5120], P('tensor', 'group'), may hold values from -0.0390625 to 0.0390625
- residual: bfloat16 [1024, 5120], P(None, 'group'), may hold values from -6 to 6
- head_grad: bfloat16 [1024, 5120], P(None, 'group'), may hold values from -6 to 6
- gain: float32 [4, 5120], replicated, may hold values from 0.1 to 1.9
- w_up: bfloat16 [5120, 55296], P(None, ('group', 'tensor')), may hold values from -0.078125 to 0.078125
- w_down: bfloat16 [55296, 5120], P(('group', 'tensor')), may hold values from -0.0546875 to 0.0546875
- route: int32 [16, 4, 24], replicated, may hold values from -1 to 63, as said below
Outputs:
- grad_hidden: bfloat16 [1024, 27648], P('group', 'tensor')
- grad_backbone: bfloat16 [27648, 5120], P('tensor', 'group')
- grad_up: bfloat16 [5120, 55296], P(None, ('group', 'tensor'))
- grad_down: bfloat16 [55296, 5120], P(('group', 'tensor'))
The draws below stay inside these ranges and needn't reach their ends.
Inputs may be any that keep to these rules, and one draw needn't show every extreme that they name: route[b, h, :] holds first the positions, within the b-th aligned block of 64 tokens, of the tokens of dataset h in that block (each position once), then -1 in the remaining slots; every token of a block belongs to exactly one dataset; in every block some dataset has exactly 24 tokens.
All inputs are finite; a program needn't handle non-finite values.
Results may differ from the reference program's by a relative error of at most 0.024.
Values may be sent and summed in bfloat16 or wider, within the bound.
A program may use at most 128 MiB of HBM per device.

```python
import jax
import jax.numpy as jnp
from jax import lax

D = 5120
FB = 27648
FF = 13824
HEADS = 4
BATCH_TOKENS = 1024
BLOCK = 64
MOST = 24


def draw_route(key, part):
    key = jax.random.fold_in(key, 7)

    def one_block(block_key):
        keys = jax.random.split(block_key, 4)
        remain = BLOCK - MOST
        first = jax.random.randint(keys[0], (), 0, MOST + 1)
        lower = jnp.maximum(0, remain - first - MOST)
        upper = jnp.minimum(MOST, remain - first)
        second = jax.random.randint(keys[1], (), lower, upper + 1)
        third = remain - first - second
        order = jax.random.permutation(keys[2], HEADS)
        sizes_list = jnp.stack([jnp.int32(MOST), first.astype(jnp.int32), second.astype(jnp.int32), third.astype(jnp.int32)])
        counts = jnp.zeros((HEADS,), jnp.int32).at[order].set(sizes_list)
        segment_starts = jnp.cumsum(counts) - counts
        shuffled = jax.random.permutation(keys[3], BLOCK).astype(jnp.int32)
        slots = jnp.arange(MOST, dtype=jnp.int32)
        index = jnp.clip(segment_starts[:, None] + slots[None, :], 0, BLOCK - 1)
        return jnp.where(slots[None, :] < counts[:, None], shuffled[index], -1).astype(jnp.int32)
    return jax.vmap(one_block)(jax.random.split(key, BATCH_TOKENS // BLOCK))


def steps_of(own_key, dims, cuts, low, top_value):
    factor_of = 1.0
    for position, parts in cuts:
        steps = jax.random.uniform(jax.random.fold_in(jax.random.fold_in(own_key, 6), position), (parts,), jnp.float32, low / len(cuts), top_value / len(cuts))
        factor_of = factor_of * jnp.repeat(jnp.exp(steps), dims[position] // parts).reshape((-1,) + (1,) * (len(dims) - 1 - position))
    return factor_of


def scatter_about(rng, extent, scale, bound, shards=(), kind=jnp.bfloat16):
    level = steps_of(rng, extent, shards, -0.22, 0.18) if shards else 1.0
    result = jax.random.normal(rng, extent, jnp.float32) * scale * level
    return jnp.minimum(jnp.maximum(result, -bound), bound).astype(kind)


def setup_inputs(seed: int = 0) -> dict:
    streams_of = jax.random.split(jax.random.key(seed), 9)
    return {
        "backbone_hidden": scatter_about(streams_of[0], (BATCH_TOKENS, FB), 1.0, 6.0, ((0, 8), (1, 16))),
        "backbone_down": scatter_about(streams_of[1], (FB, D), FB ** -0.5, 0.0390625, ((0, 16), (1, 8))),
        "residual": scatter_about(streams_of[2], (BATCH_TOKENS, D), 1.0, 6.0, ((1, 8),)),
        "head_grad": scatter_about(streams_of[3], (BATCH_TOKENS, D), 1.0, 6.0, ((1, 8),)),
        "gain": jnp.clip(1.0 + 0.18 * jax.random.normal(streams_of[4], (HEADS, D), jnp.float32), 0.1, 1.9),
        "w_up": scatter_about(streams_of[5], (D, HEADS * FF), D ** -0.5, 0.078125, ((1, 128),)),
        "w_down": scatter_about(streams_of[6], (HEADS * FF, D), FF ** -0.5, 0.0546875, ((0, 128),)),
        "route": draw_route(jax.random.fold_in(streams_of[8], 71), 0),
    }


def norm_backward(d_normed, rows_f, inv_rms, scale_row, model_width):
    scaled = d_normed * scale_row
    inner = lax.optimization_barrier(jnp.sum(rows_f * scaled, axis=-1, keepdims=True))
    return inv_rms * scaled - rows_f * inv_rms ** 3 * (inner / model_width)

def reference(backbone_hidden, backbone_down, residual, head_grad, gain, w_up, w_down, route):
    stream = (residual.astype(jnp.float32) + jnp.dot(backbone_hidden, backbone_down, preferred_element_type=jnp.float32)).astype(jnp.bfloat16)
    dataset_offsets = (jnp.arange(route.shape[0], dtype=jnp.int32) * BLOCK)[:, None]
    scattered = jnp.zeros((BATCH_TOKENS, D), jnp.float32)
    up_grads = []
    down_grads = []
    for dataset in range(HEADS):
        places = route[:, dataset, :]
        live_slot = (places >= 0).reshape(-1)
        token_index = (dataset_offsets + jnp.maximum(places, 0)).reshape(-1).astype(jnp.int32)
        head_rows = jnp.where(live_slot[:, None], stream[token_index], jnp.zeros_like(stream[token_index]))
        cot_rows = jnp.where(live_slot[:, None], head_grad[token_index], jnp.zeros_like(head_grad[token_index]))
        rows_f = head_rows.astype(jnp.float32)
        inv_rms = lax.rsqrt(lax.optimization_barrier(jnp.mean(rows_f * rows_f, axis=-1, keepdims=True)) + 1e-06)
        scale_row = gain[dataset]
        normed = (rows_f * inv_rms * scale_row).astype(jnp.bfloat16)
        up_projection_slice = w_up[:, dataset * FF:(dataset + 1) * FF]
        down_part = w_down[dataset * FF:(dataset + 1) * FF]
        pre_act = jnp.dot(normed, up_projection_slice, preferred_element_type=jnp.float32)
        sigmoid = jax.nn.sigmoid(pre_act)
        hidden_act = (pre_act * sigmoid).astype(jnp.bfloat16)
        d_act = jnp.dot(cot_rows, down_part.T, preferred_element_type=jnp.float32)
        d_pre = (d_act * sigmoid * (1.0 + pre_act * (1.0 - sigmoid))).astype(jnp.bfloat16)
        down_grads.append(jnp.dot(hidden_act.T, cot_rows, preferred_element_type=jnp.float32).astype(jnp.bfloat16))
        up_grads.append(jnp.dot(normed.T, d_pre, preferred_element_type=jnp.float32).astype(jnp.bfloat16))
        d_normed = jnp.dot(d_pre, up_projection_slice.T, preferred_element_type=jnp.float32)
        d_rows = norm_backward(d_normed, rows_f, inv_rms, scale_row, D)
        d_rows = jnp.where(live_slot[:, None], d_rows, jnp.zeros_like(d_rows))
        scattered = scattered.at[token_index].add(d_rows)
    residual_gradient = (head_grad.astype(jnp.float32) + scattered).astype(jnp.bfloat16)
    grad_backbone = jnp.dot(backbone_hidden.T, residual_gradient, preferred_element_type=jnp.float32).astype(jnp.bfloat16)
    grad_hidden = jnp.dot(residual_gradient, backbone_down.T, preferred_element_type=jnp.float32).astype(jnp.bfloat16)
    return (grad_hidden, grad_backbone, jnp.concatenate(up_grads, axis=1), jnp.concatenate(down_grads, axis=0))
```

```python
import jax
import jax.numpy as jnp
from jax import lax
from jax.experimental import pallas as pl
from jax.experimental.pallas import tpu as pltpu
from jax.sharding import PartitionSpec as P

MESH = pl.DeviceIdType.MESH
F32 = jnp.float32
BF16 = jnp.bfloat16
GROUPS = 8
ZC = 8


def place():
    g = lax.axis_index("group")
    t = lax.axis_index("tensor")
    return g // 4, g % 4, t // 8, (t // 2) % 4, t % 2


def gid(xl, y):
    return xl * 4 + lax.rem(y, 4)


def tid(xh, z, c):
    return xh * 8 + lax.rem(z, 4) * 2 + c


class Copies:
    def __init__(self, send, recv):
        self.send, self.recv, self.made = send, recv, {}

    def start(self, k, src, dst, dev):
        cp = pltpu.make_async_remote_copy(
            src_ref=src, dst_ref=dst, send_sem=self.send.at[k], recv_sem=self.recv.at[k],
            device_id=dev, device_id_type=MESH,
        )
        cp.start()
        self.made[k] = cp

    def arrived(self, *ks):
        for k in ks:
            self.made[k].wait_recv()

    def finish(self):
        for cp in self.made.values():
            cp.wait_send()


def enter(peers):
    barrier = pltpu.get_barrier_semaphore()
    for dev in peers:
        pl.semaphore_signal(barrier, inc=1, device_id=dev, device_id_type=MESH)
    pl.semaphore_wait(barrier, len(peers))


class RingGather:
    def __init__(self, buf, cps, where, half):
        xl, y, xh, z, c = where
        self.buf, self.cps, self.half = buf, cps, half
        self.g = gid(xl, y)
        self.up = (self.g, tid(xh, z + 1, c))
        self.down = (self.g, tid(xh, z + 3, c))
        self.sib = (self.g, tid(xh, z, 1 - c))
        self.me = z * 2 + c
        self.zm = lax.rem(z + 3, 4) * 2 + c
        self.zp = lax.rem(z + 1, 4) * 2 + c
        self.far = lax.rem(z + 2, 4) * 2 + c

    def begin(self):
        own = self.buf.at[self.me]
        self.cps.start(0, own, own, self.up)
        self.cps.start(1, own, own, self.down)
        self.cps.start(4, own, own, self.sib)

    def middle(self):
        (rl, cl), (rh, ch) = self.half
        self.cps.arrived(0)
        piece = self.buf.at[self.zm, rl, cl]
        self.cps.start(2, piece, piece, self.up)
        self.cps.arrived(1)
        piece = self.buf.at[self.zp, rh, ch]
        self.cps.start(3, piece, piece, self.down)
        for k, zc in ((5, self.zm), (6, self.zp)):
            self.cps.start(k, self.buf.at[zc], self.buf.at[zc], self.sib)

    def last(self):
        self.cps.arrived(2, 3)
        self.cps.start(7, self.buf.at[self.far], self.buf.at[self.far], self.sib)

    def end(self):
        self.cps.arrived(4, 5, 6, 7)


def front_kernel(
    hidden, down, resid, grad, sel, hid_out, rows_out, cots_out,
    hid, rows, cots, acc, sib_out, sib_in, z_out, z_in, x_out, x_in, pick_r, pick_c, resid_v, grad_v,
    a_s, a_r, ca_s, ca_r, cg_s, cg_r, sb_s, sb_r, z_s, z_r, x_s, x_r, ra_s, ra_r, rg_s, rg_r, local_sem,
):
    where = place()
    xl, y, xh, z, c = where
    g, t = gid(xl, y), tid(xh, z, c)
    me = z * 2 + c
    width = resid.shape[1]
    half_tok = 64

    loads = [
        pltpu.make_async_copy(hidden, hid.at[g], local_sem.at[0]),
        pltpu.make_async_copy(resid, resid_v, local_sem.at[1]),
        pltpu.make_async_copy(grad, grad_v, local_sem.at[2]),
    ]
    for cp in loads:
        cp.start()

    xp = (gid(1 - xl, y), t)
    yp, ym = (gid(xl, y + 1), t), (gid(xl, y + 3), t)
    sib = (g, tid(xh, z, 1 - c))
    xhp = (g, tid(1 - xh, z, c))
    group_peers = [(lax.rem(g + k, GROUPS), t) for k in range(1, GROUPS)]
    z_peers = [(g, tid(xh, z + k, c)) for k in range(1, 4)]
    enter(group_peers + z_peers + [sib, xhp])

    for cp in loads:
        cp.wait()

    a = Copies(a_s, a_r)
    ca = Copies(ca_s, ca_r)
    cg = Copies(cg_s, cg_r)
    sb = Copies(sb_s, sb_r)
    xx = Copies(x_s, x_r)
    ra = Copies(ra_s, ra_r)
    rg = Copies(rg_s, rg_r)

    a.start(0, hid.at[g], hid.at[g], xp)
    a.start(1, hid.at[g], hid.at[g], yp)
    a.start(2, hid.at[g], hid.at[g], ym)

    cols = pl.ds(pl.multiple_of(g * width, 128), width)

    def deal(copies, picked, buf, values):
        picked[...] = jnp.dot(sel[...], values, preferred_element_type=F32).astype(BF16).reshape(picked.shape)
        for k in range(1, GROUPS):
            to = lax.rem(g + k, GROUPS)
            copies.start(k - 1, picked.at[to // 2], buf.at[me, :, cols], (to, t))
        buf[me, :, cols] = picked[g // 2]

    deal(ca, pick_c, cots, grad_v[...])

    row_halves = (
        (slice(None), pl.ds(0, rows.shape[2] // 2)),
        (slice(None), pl.ds(rows.shape[2] // 2, rows.shape[2] // 2)),
    )
    cot_ring = RingGather(cots, cg, where, row_halves)
    row_ring = RingGather(rows, rg, where, row_halves)

    order = [
        (xl, y), (1 - xl, y), (xl, lax.rem(y + 3, 4)), (xl, lax.rem(y + 1, 4)), (xl, lax.rem(y + 2, 4)),
        (1 - xl, lax.rem(y + 3, 4)), (1 - xl, lax.rem(y + 1, 4)), (1 - xl, lax.rem(y + 2, 4)),
    ]

    def multiply(k):
        sx, sy = order[k]
        acc[k] = jnp.dot(hid[gid(sx, sy)], down[...], preferred_element_type=F32).reshape(2, half_tok, width)
        sib_out[k] = acc[k, 1 - c].astype(BF16)
        sb.start(k, sib_out.at[k], sib_in.at[k], sib)

    def z_copy(k):
        sx, sy = order[k]
        return pltpu.make_async_remote_copy(
            src_ref=z_out.at[k], dst_ref=z_in.at[sx, z], send_sem=z_s.at[k], recv_sem=z_r.at[sx, z],
            device_id=(g, tid(xh, sy, c)), device_id_type=MESH,
        )

    def pass_on(k):
        sx, sy = order[k]
        sb.arrived(k)
        z_out[k] = (acc[k, c] + sib_in[k].astype(F32)).astype(BF16)

        @pl.when(sy != z)
        def _():
            z_copy(k).start()

        @pl.when(sy == z)
        def _():
            z_in[sx, z] = z_out[k]

    multiply(0)
    a.arrived(1)
    piece = hid.at[gid(xl, y + 3), pl.ds(0, half_tok)]
    a.start(3, piece, piece, yp)
    a.arrived(2)
    piece = hid.at[gid(xl, y + 1), pl.ds(half_tok, half_tok)]
    a.start(4, piece, piece, ym)
    a.arrived(0)
    piece = hid.at[gid(1 - xl, y)]
    a.start(5, piece, piece, yp)
    a.start(6, piece, piece, ym)
    ca.arrived(*range(GROUPS - 1))
    cot_ring.begin()
    multiply(1)
    pass_on(0)
    multiply(2)
    pass_on(1)
    multiply(3)
    pass_on(2)
    a.arrived(3, 4)
    piece = hid.at[gid(xl, y + 2)]
    a.start(7, piece, piece, xp)
    multiply(4)
    pass_on(3)
    cot_ring.middle()
    pass_on(4)
    a.arrived(5)
    multiply(5)
    a.arrived(6)
    multiply(6)
    pass_on(5)
    pass_on(6)
    a.arrived(7)
    multiply(7)
    pass_on(7)
    hid_cp = pltpu.make_async_copy(hid, hid_out, local_sem.at[0])
    hid_cp.start()

    for sx in range(2):
        for dz in range(1, 4):
            src = lax.rem(z + dz, 4)
            pltpu.make_async_remote_copy(
                src_ref=z_out.at[0], dst_ref=z_in.at[sx, src], send_sem=z_s.at[0], recv_sem=z_r.at[sx, src],
                device_id=(g, tid(xh, z + dz, c)), device_id_type=MESH,
            ).wait_recv()
    parts = z_in[...].astype(F32)
    x_out[...] = ((parts[:, 0] + parts[:, 1]) + (parts[:, 2] + parts[:, 3])).astype(BF16)
    xx.start(0, x_out, x_in, xhp)
    cot_ring.last()
    xx.arrived(0)
    total = (x_out[...].astype(F32) + x_in[...].astype(F32)).reshape(2 * half_tok, width)
    stream = (resid_v[...].astype(F32) + total).astype(BF16)
    deal(ra, pick_r, rows, stream)
    ra.arrived(*range(GROUPS - 1))
    row_ring.begin()
    cot_ring.end()
    cot_cp = pltpu.make_async_copy(cots, cots_out, local_sem.at[1])
    cot_cp.start()
    row_ring.middle()
    row_ring.last()
    row_ring.end()
    row_cp = pltpu.make_async_copy(rows, rows_out, local_sem.at[2])
    row_cp.start()

    for cps in (a, ca, cg, sb, xx, ra, rg):
        cps.finish()
    for k in range(GROUPS):
        @pl.when(order[k][1] != z)
        def _():
            z_copy(k).wait_send()
    hid_cp.wait()
    cot_cp.wait()
    row_cp.wait()


def front(hidden, down, resid, grad, sel):
    tokens, inner = hidden.shape
    width = down.shape[1]
    slots = sel.shape[0] // 4
    model = width * GROUPS
    any_spec = pl.BlockSpec(memory_space=pl.ANY)
    vmem = pl.BlockSpec(memory_space=pltpu.VMEM)
    dma = pltpu.SemaphoreType.DMA
    sems = []
    for n in (8, 7, 8, 8):
        sems += [dma((n,)), dma((n,))]
    sems += [dma((8,)), dma((2, 4)), dma((1,)), dma((1,)), dma((7,)), dma((7,)), dma((8,)), dma((8,)), dma((3,))]
    return pl.pallas_call(
        front_kernel,
        out_shape=(
            jax.ShapeDtypeStruct((GROUPS, tokens, inner), BF16),
            jax.ShapeDtypeStruct((ZC, slots, model), BF16),
            jax.ShapeDtypeStruct((ZC, slots, model), BF16),
        ),
        in_specs=[any_spec, vmem, any_spec, any_spec, vmem],
        out_specs=(any_spec, any_spec, any_spec),
        scratch_shapes=[
            pltpu.VMEM((GROUPS, tokens, inner), BF16),
            pltpu.VMEM((ZC, slots, model), BF16),
            pltpu.VMEM((ZC, slots, model), BF16),
            pltpu.VMEM((8, 2, 64, width), F32),
            pltpu.VMEM((8, 64, width), BF16),
            pltpu.VMEM((8, 64, width), BF16),
            pltpu.VMEM((8, 64, width), BF16),
            pltpu.VMEM((2, 4, 64, width), BF16),
            pltpu.VMEM((2, 64, width), BF16),
            pltpu.VMEM((2, 64, width), BF16),
            pltpu.VMEM((4, slots, width), BF16),
            pltpu.VMEM((4, slots, width), BF16),
            pltpu.VMEM((128, width), BF16),
            pltpu.VMEM((128, width), BF16),
        ] + sems,
        compiler_params=pltpu.CompilerParams(
            collective_id=0, has_side_effects=True, vmem_limit_bytes=56 * 1024 * 1024
        ),
        name="front",
    )(hidden, down, resid, grad, sel)


def norm_backward(d_normed, rows_f, inv_rms, scale_row, model_width):
    scaled = d_normed * scale_row
    inner = jnp.sum(rows_f * scaled, axis=-1, keepdims=True)
    return inv_rms * scaled - rows_f * inv_rms**3 * (inner / model_width)


def local(backbone_hidden, backbone_down, residual, head_grad, gain, w_up, w_down, route):
    groups = lax.axis_size("group")
    head_count = gain.shape[0]
    model_width = gain.shape[1]
    pair_size = groups // head_count
    dataset = lax.axis_index("group") // pair_size
    zc = lax.rem(lax.axis_index("tensor"), 8)
    blocks = route.shape[0]
    slot_count = route.shape[2]
    tokens = residual.shape[0]
    block_len = tokens // blocks
    slice_width = residual.shape[1]

    def mine(a):
        pair = a.reshape((2, 8) + a.shape[1:])
        return lax.dynamic_index_in_dim(pair, zc, 1, keepdims=False)

    own_route = mine(route)
    resid = mine(residual.reshape(blocks, block_len, slice_width)).reshape(2 * block_len, slice_width)
    grad = mine(head_grad.reshape(blocks, block_len, slice_width)).reshape(2 * block_len, slice_width)
    wanted = jnp.where(own_route >= 0, own_route + (jnp.arange(2, dtype=jnp.int32) * block_len)[:, None, None], -1)
    wanted = wanted.transpose(1, 0, 2).reshape(head_count * 2 * slot_count)
    sel = (wanted[:, None] == jnp.arange(2 * block_len, dtype=jnp.int32)[None]).astype(BF16)

    hidden_all, rows8, cots8 = front(backbone_hidden, backbone_down, resid, grad, sel)
    hidden_all = hidden_all.reshape(tokens, -1)

    def by_block(a):
        return a.reshape(8, 2, slot_count, model_width).transpose(1, 0, 2, 3).reshape(blocks * slot_count, model_width)

    head_rows, cot_rows = by_block(rows8), by_block(cots8)
    places = lax.broadcasted_iota(jnp.int32, (blocks, head_count, slot_count, block_len), 3)
    dataset_selector = route[:, :, :, None] == places
    rows_f = head_rows.astype(jnp.float32)
    inv_rms = lax.rsqrt(jnp.mean(rows_f * rows_f, axis=-1, keepdims=True) + 1e-06)
    scale_row = lax.dynamic_index_in_dim(gain, dataset, 0, keepdims=False)
    normed = (rows_f * inv_rms * scale_row).astype(jnp.bfloat16)
    pre_act = jnp.dot(normed, w_up, preferred_element_type=jnp.float32)
    sigmoid = jax.nn.sigmoid(pre_act)
    hidden_act = (pre_act * sigmoid).astype(jnp.bfloat16)
    d_act = lax.dot_general(
        cot_rows, w_down, (((1,), (1,)), ((), ())), preferred_element_type=jnp.float32
    )
    d_pre = (d_act * sigmoid * (1.0 + pre_act * (1.0 - sigmoid))).astype(jnp.bfloat16)
    grad_down = lax.dot_general(
        hidden_act, cot_rows, (((0,), (0,)), ((), ())), preferred_element_type=jnp.float32
    ).astype(jnp.bfloat16)
    grad_up = lax.dot_general(
        normed, d_pre, (((0,), (0,)), ((), ())), preferred_element_type=jnp.float32
    ).astype(jnp.bfloat16)
    d_normed = lax.dot_general(
        d_pre, w_up, (((1,), (1,)), ((), ())), preferred_element_type=jnp.float32
    )
    d_summed = lax.psum(d_normed.astype(jnp.bfloat16), "tensor").astype(jnp.float32)
    d_rows = norm_backward(d_summed, rows_f, inv_rms, scale_row, model_width)
    returned_rows = lax.all_to_all(
        d_rows.astype(jnp.bfloat16), "group", split_axis=1, concat_axis=0, tiled=True
    ).astype(d_rows.dtype)
    returned_rows = returned_rows.reshape(
        head_count, pair_size, blocks, slot_count, slice_width
    ).sum(axis=1)
    scattered = jnp.einsum(
        "lret,rlez->ltz",
        dataset_selector.astype(jnp.float32),
        returned_rows,
        precision=lax.Precision.HIGHEST,
    )
    residual_gradient = (
        head_grad.astype(jnp.float32) + scattered.reshape(tokens, slice_width)
    ).astype(jnp.bfloat16)
    grad_backbone = lax.dot_general(
        hidden_all, residual_gradient, (((0,), (0,)), ((), ())), preferred_element_type=jnp.float32
    ).astype(jnp.bfloat16)
    grad_hidden = lax.psum_scatter(
        lax.dot_general(
            residual_gradient,
            backbone_down,
            (((1,), (1,)), ((), ())),
            preferred_element_type=jnp.float32,
        ).astype(jnp.bfloat16),
        "group",
        scatter_dimension=0,
        tiled=True,
    )
    return (grad_hidden, grad_backbone, grad_up, grad_down)


def solution(mesh):
    placed = (
        P("group", "tensor"),
        P("tensor", "group"),
        P(None, "group"),
        P(None, "group"),
        P(),
        P(None, ("group", "tensor")),
        P(("group", "tensor"), None),
        P(),
    )
    return jax.shard_map(
        local,
        mesh=mesh,
        in_specs=placed,
        out_specs=(
            P("group", "tensor"),
            P("tensor", "group"),
            P(None, ("group", "tensor")),
            P(("group", "tensor"), None),
        ),
        check_vma=False,
    )
```

```python
import jax
import jax.numpy as jnp
from jax import lax
from jax.experimental import pallas as pl
from jax.experimental.pallas import tpu as pltpu
from jax.sharding import PartitionSpec as P

MESH = pl.DeviceIdType.MESH
F32 = jnp.float32
BF16 = jnp.bfloat16
GROUPS = 8
ZC = 8


def place():
    g = lax.axis_index("group")
    t = lax.axis_index("tensor")
    return g // 4, g % 4, t // 8, (t // 2) % 4, t % 2


def gid(xl, y):
    return xl * 4 + lax.rem(y, 4)


def tid(xh, z, c):
    return xh * 8 + lax.rem(z, 4) * 2 + c


class Copies:
    def __init__(self, send, recv):
        self.send, self.recv, self.made = send, recv, {}

    def start(self, k, src, dst, dev):
        cp = pltpu.make_async_remote_copy(
            src_ref=src, dst_ref=dst, send_sem=self.send.at[k], recv_sem=self.recv.at[k],
            device_id=dev, device_id_type=MESH,
        )
        cp.start()
        self.made[k] = cp

    def arrived(self, *ks):
        for k in ks:
            self.made[k].wait_recv()

    def finish(self):
        for cp in self.made.values():
            cp.wait_send()


def enter(peers):
    barrier = pltpu.get_barrier_semaphore()
    for dev in peers:
        pl.semaphore_signal(barrier, inc=1, device_id=dev, device_id_type=MESH)
    pl.semaphore_wait(barrier, len(peers))


class RingGather:
    def __init__(self, buf, cps, where, half):
        xl, y, xh, z, c = where
        self.buf, self.cps, self.half = buf, cps, half
        self.g = gid(xl, y)
        self.up = (self.g, tid(xh, z + 1, c))
        self.down = (self.g, tid(xh, z + 3, c))
        self.sib = (self.g, tid(xh, z, 1 - c))
        self.me = z * 2 + c
        self.zm = lax.rem(z + 3, 4) * 2 + c
        self.zp = lax.rem(z + 1, 4) * 2 + c
        self.far = lax.rem(z + 2, 4) * 2 + c

    def begin(self):
        own = self.buf.at[self.me]
        self.cps.start(0, own, own, self.up)
        self.cps.start(1, own, own, self.down)
        self.cps.start(4, own, own, self.sib)

    def middle(self):
        (rl, cl), (rh, ch) = self.half
        self.cps.arrived(0)
        piece = self.buf.at[self.zm, rl, cl]
        self.cps.start(2, piece, piece, self.up)
        self.cps.arrived(1)
        piece = self.buf.at[self.zp, rh, ch]
        self.cps.start(3, piece, piece, self.down)
        for k, zc in ((5, self.zm), (6, self.zp)):
            self.cps.start(k, self.buf.at[zc], self.buf.at[zc], self.sib)

    def last(self):
        self.cps.arrived(2, 3)
        self.cps.start(7, self.buf.at[self.far], self.buf.at[self.far], self.sib)

    def end(self):
        self.cps.arrived(4, 5, 6, 7)

NT = (((1,), (1,)), ((), ()))
TN = (((0,), (0,)), ((), ()))


def kernel(
    hidden_t, down_h, resid, grad, gain, w_up_t, w_down, sel, sel_back,
    gh_out, gb_out, gu_out, gd_out,
    hid, down, wu, wd, rows, cots, normed,
    acc, sib_out, sib_in, z_out, z_in, x_out, x_in, pick_r, pick_c, resid_v, grad_v,
    pre, dact, act_t, dpre_t, dpre,
    stage, dn, sd_out, sd_in, far_out, far_in, dir_out, dir_in, sum_out, sum_in,
    tot, drow, back_in, x2_out, x2_in, ds, fp, fin, fhalf, gh_v,
    a_s, a_r, ca_s, ca_r, cg_s, cg_r, sb_s, sb_r, z_s, z_r, x_s, x_r, ra_s, ra_r, rg_s, rg_r,
    sd_s, sd_r, fr_s, fr_r, nd_s, nd_r, ns_s, ns_r, ba_s, ba_r, x2_s, x2_r, dg_s, dg_r, f_s, f_r, local_sem,
):
    where = place()
    xl, y, xh, z, c = where
    g, t = gid(xl, y), tid(xh, z, c)
    me = z * 2 + c
    head = g // 2
    width = resid.shape[1]
    model = rows.shape[2]
    inner = hid.shape[1]
    slots = rows.shape[1]
    part = inner // 2

    loads = [pltpu.make_async_copy(hidden_t, hid.at[g], local_sem.at[0])]
    for i in range(2):
        tok = pl.ds(pl.multiple_of((8 * i + me) * 64, 64), 64)
        loads.append(pltpu.make_async_copy(grad.at[tok], grad_v.at[pl.ds(64 * i, 64)], local_sem.at[1 + i]))
        loads.append(pltpu.make_async_copy(resid.at[tok], resid_v.at[pl.ds(64 * i, 64)], local_sem.at[3 + i]))
    late = [
        pltpu.make_async_copy(down_h, down, local_sem.at[5]),
        pltpu.make_async_copy(w_down, wd, local_sem.at[6]),
        pltpu.make_async_copy(w_up_t, wu, local_sem.at[7]),
    ]
    for cp in loads:
        cp.start()

    xp = (gid(1 - xl, y), t)
    yp, ym = (gid(xl, y + 1), t), (gid(xl, y + 3), t)
    sib = (g, tid(xh, z, 1 - c))
    xhp = (g, tid(1 - xh, z, c))
    zup, zdown = (g, tid(xh, z + 1, c)), (g, tid(xh, z + 3, c))
    group_peers = [(lax.rem(g + k, GROUPS), t) for k in range(1, GROUPS)]
    z_peers = [(g, tid(xh, z + k, c)) for k in range(1, 4)]
    with jax.named_scope("enter"):
        enter(group_peers + z_peers + [sib, xhp])
        for cp in loads:
            cp.wait()

    a, ca, cg, sb = Copies(a_s, a_r), Copies(ca_s, ca_r), Copies(cg_s, cg_r), Copies(sb_s, sb_r)
    xx, ra, rg = Copies(x_s, x_r), Copies(ra_s, ra_r), Copies(rg_s, rg_r)
    sd, fr, nd, ns = Copies(sd_s, sd_r), Copies(fr_s, fr_r), Copies(nd_s, nd_r), Copies(ns_s, ns_r)
    ba, x2, dg, f = Copies(ba_s, ba_r), Copies(x2_s, x2_r), Copies(dg_s, dg_r), Copies(f_s, f_r)

    a.start(0, hid.at[g], hid.at[g], xp)
    a.start(1, hid.at[g], hid.at[g], yp)
    a.start(2, hid.at[g], hid.at[g], ym)
    for cp in late:
        cp.start()

    def cols(j):
        return pl.ds(pl.multiple_of(j * width, 128), width)

    def deal(copies, picked, buf, values):
        picked[...] = jnp.dot(sel[...], values, preferred_element_type=F32).astype(BF16).reshape(picked.shape)
        for k in range(1, GROUPS):
            to = lax.rem(g + k, GROUPS)
            copies.start(k - 1, picked.at[to // 2], buf.at[me, :, cols(g)], (to, t))
        buf[me, :, cols(g)] = picked[head]

    deal(ca, pick_c, cots, grad_v[...])

    row_halves = (
        (slice(None), pl.ds(0, model // 2)),
        (slice(None), pl.ds(model // 2, model // 2)),
    )
    tok_halves = ((pl.ds(0, 64), slice(None)), (pl.ds(64, 64), slice(None)))
    cot_ring = RingGather(cots, cg, where, row_halves)
    row_ring = RingGather(rows, rg, where, row_halves)
    ds_ring = RingGather(ds, dg, where, tok_halves)

    order = [
        (xl, y), (1 - xl, y), (xl, lax.rem(y + 3, 4)), (xl, lax.rem(y + 1, 4)), (xl, lax.rem(y + 2, 4)),
        (1 - xl, lax.rem(y + 3, 4)), (1 - xl, lax.rem(y + 1, 4)), (1 - xl, lax.rem(y + 2, 4)),
    ]

    def multiply(k):
        sx, sy = order[k]
        acc[k] = lax.dot_general(hid[gid(sx, sy)], down[...], TN, preferred_element_type=F32).reshape(2, 64, width)
        sib_out[k] = acc[k, 1 - c].astype(BF16)
        sb.start(k, sib_out.at[k], sib_in.at[k], sib)

    def z_copy(k):
        sx, sy = order[k]
        return pltpu.make_async_remote_copy(
            src_ref=z_out.at[k], dst_ref=z_in.at[sx, z], send_sem=z_s.at[k], recv_sem=z_r.at[sx, z],
            device_id=(g, tid(xh, sy, c)), device_id_type=MESH,
        )

    def pass_on(k):
        sx, sy = order[k]
        sb.arrived(k)
        z_out[k] = (acc[k, c] + sib_in[k].astype(F32)).astype(BF16)

        @pl.when(sy != z)
        def _():
            z_copy(k).start()

        @pl.when(sy == z)
        def _():
            z_in[sx, z] = z_out[k]

    k_step = 1024

    def product(total, weights, values, lo, hi):
        @pl.loop(lo, hi)
        def _(k):
            kc = pl.ds(pl.multiple_of(k * k_step, 128), k_step)
            term = lax.dot_general(
                weights[:, kc], values[:, :, kc].reshape(ZC * slots, k_step), NT, preferred_element_type=F32
            )
            total[...] += term

    with jax.named_scope("gather_hidden"):
        late[0].wait()
        multiply(0)
        a.arrived(1)
        piece = hid.at[gid(xl, y + 3), pl.ds(0, part)]
        a.start(3, piece, piece, yp)
        a.arrived(2)
        piece = hid.at[gid(xl, y + 1), pl.ds(part, part)]
        a.start(4, piece, piece, ym)
        a.arrived(0)
        piece = hid.at[gid(1 - xl, y)]
        a.start(5, piece, piece, yp)
        a.start(6, piece, piece, ym)
        ca.arrived(*range(GROUPS - 1))
        cot_ring.begin()
        multiply(1)
        pass_on(0)
        multiply(2)
        pass_on(1)
        multiply(3)
        pass_on(2)
        a.arrived(3, 4)
        piece = hid.at[gid(xl, y + 2)]
        a.start(7, piece, piece, xp)
        multiply(4)
        pass_on(3)
        pass_on(4)
    with jax.named_scope("gather_cots"):
        cot_ring.middle()
        pre[...] = jnp.zeros_like(pre)
        dact[...] = jnp.zeros_like(dact)
    with jax.named_scope("gather_rest"):
        a.arrived(5)
        multiply(5)
        a.arrived(6)
        multiply(6)
        pass_on(5)
        pass_on(6)
        a.arrived(7)
        multiply(7)
        pass_on(7)
    with jax.named_scope("sum_stream"):
        cot_ring.last()
        for sx in range(2):
            for dz in range(1, 4):
                src = lax.rem(z + dz, 4)
                pltpu.make_async_remote_copy(
                    src_ref=z_out.at[0], dst_ref=z_in.at[sx, src], send_sem=z_s.at[0], recv_sem=z_r.at[sx, src],
                    device_id=(g, tid(xh, z + dz, c)), device_id_type=MESH,
                ).wait_recv()
        parts = z_in[...].astype(F32)
        x_out[...] = ((parts[:, 0] + parts[:, 1]) + (parts[:, 2] + parts[:, 3])).astype(BF16)
        xx.start(0, x_out, x_in, xhp)
        xx.arrived(0)
        total = (x_out[...].astype(F32) + x_in[...].astype(F32)).reshape(2 * 64, width)
        stream = (resid_v[...].astype(F32) + total).astype(BF16)
    with jax.named_scope("deal_rows"):
        deal(ra, pick_r, rows, stream)
        ra.arrived(*range(GROUPS - 1))
        row_ring.begin()

    def gain_at(j):
        return gain[pl.ds(head, 1), cols(j)]

    def norm_shard(zc):
        def add(j, squares):
            v = rows[zc, :, cols(j)].astype(F32)
            return squares + v * v

        squares = lax.fori_loop(0, GROUPS, add, jnp.zeros((slots, width), F32))
        inv = lax.rsqrt(jnp.sum(squares, axis=-1, keepdims=True) * (1.0 / model) + 1e-06)

        @pl.loop(0, GROUPS)
        def _(j):
            v = rows[zc, :, cols(j)].astype(F32)
            normed[zc, :, cols(j)] = (v * inv * gain_at(j)).astype(BF16)

        return inv

    with jax.named_scope("gather_rows"):
        cot_ring.end()
        late[1].wait()
        late[2].wait()
        inv_own = norm_shard(me)
        product(dact, wd, cots, 0, 5)
        row_ring.middle()
        row_ring.cps.arrived(4)
        norm_shard(z * 2 + 1 - c)
        norm_shard(row_ring.zm)
        norm_shard(row_ring.zp)
        row_ring.cps.arrived(5, 6)
        norm_shard(lax.rem(z + 3, 4) * 2 + 1 - c)
        norm_shard(lax.rem(z + 1, 4) * 2 + 1 - c)
        row_ring.last()
        norm_shard(row_ring.far)
        row_ring.cps.arrived(7)
        norm_shard(lax.rem(z + 2, 4) * 2 + 1 - c)

    with jax.named_scope("heads"):
        product(pre, wu, normed, 0, 5)

        @pl.loop(0, pre.shape[0] // 48)
        def _(i):
            r = pl.ds(pl.multiple_of(i * 48, 16), 48)
            p = pre[r, :]
            s = jax.nn.sigmoid(p)
            act_t[r, :] = (p * s).astype(BF16)
            dpre_t[r, :] = (dact[r, :] * s * (1.0 + p * (1.0 - s))).astype(BF16)

        dpre[...] = dpre_t[...].T

    def dn_multiply(j):
        stage[...] = jnp.dot(dpre[...], wu[:, cols(j)], preferred_element_type=F32).reshape(stage.shape)
        dn[j] = stage[:, c]
        sd_out[j] = stage[:, 1 - c].astype(BF16)
        sd.start(j, sd_out.at[j], sd_in.at[j], sib)

    def toward(j):
        return (zup, zdown, lax.rem(z + 1, 4), lax.rem(z + 3, 4)) if j < 4 else (
            zdown, zup, lax.rem(z + 3, 4), lax.rem(z + 1, 4))

    def dn_split(j):
        to, other, z_to, z_other = toward(j)
        sd.arrived(j)
        dn[j] = dn[j] + sd_in[j].astype(F32)
        far_out[j] = dn[j, lax.rem(z + 2, 4)].astype(BF16)
        fr.start(j, far_out.at[j], far_in.at[j], to)
        dir_out[j] = dn[j, z_other].astype(BF16)
        nd.start(j, dir_out.at[j], dir_in.at[j], other)

    def dn_forward(j):
        to, other, z_to, z_other = toward(j)
        fr.arrived(j)
        sum_out[j] = (dn[j, z_to] + far_in[j].astype(F32)).astype(BF16)
        ns.start(j, sum_out.at[j], sum_in.at[j], to)

    js = [0, 4, 1, 5, 2, 6, 3, 7]
    with jax.named_scope("row_gradients"):
        for i in range(len(js) + 3):
            if i < 8:
                dn_multiply(js[i])
            if 0 <= i - 1 < 8:
                dn_split(js[i - 1])
            if 0 <= i - 3 < 8:
                dn_forward(js[i - 3])

    def down_grad(j):
        wd[:, cols(j)] = jnp.dot(
            act_t[...], cots[:, :, cols(j)].reshape(ZC * slots, width), preferred_element_type=F32
        ).astype(BF16)

    def up_grad(j):
        wu[:, cols(j)] = jnp.dot(
            dpre_t[...], normed[:, :, cols(j)].reshape(ZC * slots, width), preferred_element_type=F32
        ).astype(BF16)

    with jax.named_scope("down_grads"):
        pl.loop(0, GROUPS)(down_grad)
        gd_copy = pltpu.make_async_copy(wd, gd_out, local_sem.at[0])
        gd_copy.start()

    with jax.named_scope("norm_backward"):
        dot_sum = jnp.zeros((slots, width), F32)
        for j in js:
            ns.arrived(j)
            nd.arrived(j)
            q = (dn[j, z] + sum_in[j].astype(F32) + dir_in[j].astype(F32)) * gain_at(j)
            tot[j] = q
            dot_sum = dot_sum + q * rows[me, :, cols(j)].astype(F32)
        back = inv_own * inv_own * inv_own * (jnp.sum(dot_sum, axis=-1, keepdims=True) * (1.0 / model))

        @pl.loop(0, GROUPS)
        def _(j):
            drow[j] = (inv_own * tot[j] - rows[me, :, cols(j)].astype(F32) * back).astype(BF16)

        for k in range(1, GROUPS):
            to = lax.rem(g + k, GROUPS)
            ba.start(k - 1, drow.at[to], back_in.at[g], (to, t))
        back_in[g] = drow[g]

    with jax.named_scope("return_rows"):
        pl.loop(0, 3)(up_grad)
        ba.arrived(*range(GROUPS - 1))
        x2_out[...] = jnp.dot(
            sel_back[...], back_in[...].reshape(GROUPS * slots, width), preferred_element_type=F32
        ).astype(BF16)
        x2.start(0, x2_out, x2_in, xhp)
        x2.arrived(0)
        ds[me] = (grad_v[...].astype(F32) + (x2_out[...].astype(F32) + x2_in[...].astype(F32))).astype(BF16)
        ds_ring.begin()
    with jax.named_scope("gather_dstream"):
        pl.loop(3, GROUPS)(up_grad)
        gu_copy = pltpu.make_async_copy(wu, gu_out, local_sem.at[1])
        gu_copy.start()
        ds_ring.middle()
        ds_ring.last()
        ds_ring.end()

    def tokens_of(sx, sy):
        at = pl.ds(pl.multiple_of(sx * 64, 64), 64)
        return [ds[sy * 2, at, :], ds[sy * 2 + 1, at, :]]

    m_step = inner // 4

    def hidden_grads(i, first, second):
        both = jnp.concatenate(tokens_of(*first) + tokens_of(*second), axis=0)

        @pl.loop(0, 4)
        def _(m):
            r = pl.ds(pl.multiple_of(m * m_step, 16), m_step)
            p = lax.dot_general(down[r, :], both, NT, preferred_element_type=F32).astype(BF16)
            fp[i, r, :] = p[:, :128]
            fp[i + 1, r, :] = p[:, 128:]

    y1, y2, y3 = lax.rem(y + 1, 4), lax.rem(y + 2, 4), lax.rem(y + 3, 4)
    low, high = pl.ds(0, part), pl.ds(part, part)

    def add_into(dst, *terms):
        total = dst[...].astype(F32)
        for term in terms:
            total = total + term[...].astype(F32)
        return total.astype(BF16)

    with jax.named_scope("hidden_grads"):
        hidden_grads(2, (1 - xl, y1), (1 - xl, y3))
        f.start(0, fp.at[2], fin.at[0], yp)
        f.start(1, fp.at[3], fin.at[1], ym)
        hidden_grads(0, (1 - xl, y2), (xl, y2))
        f.start(2, fp.at[0], fin.at[2], xp)
        hidden_grads(4, (xl, y1), (xl, y3))
        f.start(3, fp.at[4, high], fin.at[3, high], yp)
        f.start(4, fp.at[5, low], fin.at[4, low], ym)
        hidden_grads(6, (1 - xl, y), (xl, y))

    def backbone_grad(m):
        r = pl.ds(pl.multiple_of(m * m_step, 16), m_step)
        total = jnp.zeros((m_step, width), F32)
        for i in range(4):
            left = jnp.concatenate([hid[2 * i, r, :], hid[2 * i + 1, r, :]], axis=1)
            right = jnp.concatenate(
                tokens_of((2 * i) // 4, (2 * i) % 4) + tokens_of((2 * i + 1) // 4, (2 * i + 1) % 4), axis=0)
            total = total + jnp.dot(left, right, preferred_element_type=F32)
        down[r, :] = total.astype(BF16)

    with jax.named_scope("sum_hidden_grads"):
        f.arrived(2)
        fp[1] = add_into(fp.at[1], fin.at[2])
        f.start(5, fp.at[1, low], fhalf.at[0], yp)
        f.start(6, fp.at[1, high], fhalf.at[1], ym)
        f.arrived(0, 1)
        fp[6] = add_into(fp.at[6], fin.at[0], fin.at[1])
        f.start(7, fp.at[6], fin.at[5], xp)
        pl.loop(0, 4)(backbone_grad)
        gb_copy = pltpu.make_async_copy(down, gb_out, local_sem.at[2])
        gb_copy.start()
        f.arrived(5)
        fp[4, low] = add_into(fp.at[4, low], fhalf.at[0])
        f.start(8, fp.at[4, low], fin.at[3, low], yp)
        f.arrived(6)
        fp[5, high] = add_into(fp.at[5, high], fhalf.at[1])
        f.start(9, fp.at[5, high], fin.at[4, high], ym)
        f.arrived(7)
        fp[7] = add_into(fp.at[7], fin.at[5])
        f.arrived(3, 4, 8, 9)
        gh_v[...] = add_into(fp.at[7], fin.at[3], fin.at[4])
        gh_copy = pltpu.make_async_copy(gh_v, gh_out, local_sem.at[3])
        gh_copy.start()

    with jax.named_scope("finish"):
        for cps in (a, ca, cg, sb, xx, ra, rg, sd, fr, nd, ns, ba, x2, dg, f):
            cps.finish()
        for k in range(GROUPS):
            @pl.when(order[k][1] != z)
            def _():
                z_copy(k).wait_send()
        for cp in (gd_copy, gu_copy, gb_copy, gh_copy):
            cp.wait()


def run(hidden_t, down, resid, grad, gain, w_up_t, w_down, sel, sel_back):
    inner, tokens = hidden_t.shape
    width = down.shape[1]
    slots = sel.shape[0] // 4
    model = width * GROUPS
    units = w_down.shape[0]
    any_spec = pl.BlockSpec(memory_space=pl.ANY)
    vmem = pl.BlockSpec(memory_space=pltpu.VMEM)
    dma = pltpu.SemaphoreType.DMA
    sems = []
    for n in ((8,), (7,), (8,), (8,)):
        sems += [dma(n), dma(n)]
    sems += [dma((8,)), dma((2, 4))]
    for n in ((1,), (7,), (8,), (8,), (8,), (8,), (8,), (7,), (1,), (8,), (10,)):
        sems += [dma(n), dma(n)]
    sems += [dma((8,))]
    piece = (64, width)
    return pl.pallas_call(
        kernel,
        out_shape=(
            jax.ShapeDtypeStruct((inner, tokens), BF16),
            jax.ShapeDtypeStruct((inner, width), BF16),
            jax.ShapeDtypeStruct((units, model), BF16),
            jax.ShapeDtypeStruct((units, model), BF16),
        ),
        in_specs=[any_spec] * 4 + [vmem] + [any_spec] * 2 + [vmem] * 2,
        out_specs=(any_spec,) * 4,
        scratch_shapes=[
            pltpu.VMEM((GROUPS, inner, tokens), BF16),
            pltpu.VMEM((inner, width), BF16),
            pltpu.VMEM((units, model), BF16),
            pltpu.VMEM((units, model), BF16),
            pltpu.VMEM((ZC, slots, model), BF16),
            pltpu.VMEM((ZC, slots, model), BF16),
            pltpu.VMEM((ZC, slots, model), BF16),
            pltpu.VMEM((8, 2) + piece, F32),
            pltpu.VMEM((8,) + piece, BF16),
            pltpu.VMEM((8,) + piece, BF16),
            pltpu.VMEM((8,) + piece, BF16),
            pltpu.VMEM((2, 4) + piece, BF16),
            pltpu.VMEM((2,) + piece, BF16),
            pltpu.VMEM((2,) + piece, BF16),
            pltpu.VMEM((4, slots, width), BF16),
            pltpu.VMEM((4, slots, width), BF16),
            pltpu.VMEM((128, width), BF16),
            pltpu.VMEM((128, width), BF16),
            pltpu.VMEM((units, ZC * slots), F32),
            pltpu.VMEM((units, ZC * slots), F32),
            pltpu.VMEM((units, ZC * slots), BF16),
            pltpu.VMEM((units, ZC * slots), BF16),
            pltpu.VMEM((ZC * slots, units), BF16),
            pltpu.VMEM((4, 2, slots, width), F32),
            pltpu.VMEM((8, 4, slots, width), F32),
            pltpu.VMEM((8, 4, slots, width), BF16),
            pltpu.VMEM((8, 4, slots, width), BF16),
        ]
        + [pltpu.VMEM((8, slots, width), BF16)] * 6
        + [
            pltpu.VMEM((8, slots, width), F32),
            pltpu.VMEM((8, slots, width), BF16),
            pltpu.VMEM((8, slots, width), BF16),
            pltpu.VMEM((128, width), BF16),
            pltpu.VMEM((128, width), BF16),
            pltpu.VMEM((8, 128, width), BF16),
            pltpu.VMEM((8, inner, tokens), BF16),
            pltpu.VMEM((6, inner, tokens), BF16),
            pltpu.VMEM((2, inner // 2, tokens), BF16),
            pltpu.VMEM((inner, tokens), BF16),
        ]
        + sems,
        compiler_params=pltpu.CompilerParams(
            collective_id=0, has_side_effects=True, vmem_limit_bytes=62 * 1024 * 1024
        ),
        name="backbone_and_heads",
    )(hidden_t, down, resid, grad, gain, w_up_t, w_down, sel, sel_back)


def local(backbone_hidden, backbone_down, residual, head_grad, gain, w_up, w_down, route):
    groups = lax.axis_size("group")
    heads = gain.shape[0]
    zc = lax.rem(lax.axis_index("tensor"), ZC)
    blocks, _, slot_count = route.shape
    block_len = residual.shape[0] // blocks
    own = lax.dynamic_index_in_dim(route.reshape(2, ZC, heads, slot_count), zc, 1, keepdims=False)
    wanted = jnp.where(own >= 0, own + (jnp.arange(2, dtype=jnp.int32) * block_len)[:, None, None], -1)
    wanted = wanted.transpose(1, 0, 2).reshape(heads, 2 * slot_count)
    positions = jnp.arange(2 * block_len, dtype=jnp.int32)
    sel = (wanted.reshape(-1)[:, None] == positions[None]).astype(BF16)
    twice = jnp.repeat(wanted, groups // heads, axis=0).reshape(-1)
    sel_back = (positions[:, None] == twice[None]).astype(BF16)
    gh, gb, gu, gd = run(
        backbone_hidden.T, backbone_down, residual, head_grad, gain, w_up.T, w_down, sel, sel_back
    )
    return (gh.T, gb, gu.T, gd)


def solution(mesh):
    placed = (
        P("group", "tensor"),
        P("tensor", "group"),
        P(None, "group"),
        P(None, "group"),
        P(),
        P(None, ("group", "tensor")),
        P(("group", "tensor"), None),
        P(),
    )
    return jax.shard_map(
        local,
        mesh=mesh,
        in_specs=placed,
        out_specs=(
            P("group", "tensor"),
            P("tensor", "group"),
            P(None, ("group", "tensor")),
            P(("group", "tensor"), None),
        ),
        check_vma=False,
    )
```

```python
import jax
import jax.numpy as jnp
from jax import lax
from jax.experimental import pallas as pl
from jax.experimental.pallas import tpu as pltpu
from jax.sharding import PartitionSpec as P

MESH = pl.DeviceIdType.MESH
F32 = jnp.float32
BF16 = jnp.bfloat16
GROUPS = 8
ZC = 8


def place():
    g = lax.axis_index("group")
    t = lax.axis_index("tensor")
    return g // 4, g % 4, t // 8, (t // 2) % 4, t % 2


def gid(xl, y):
    return xl * 4 + lax.rem(y, 4)


def tid(xh, z, c):
    return xh * 8 + lax.rem(z, 4) * 2 + c


class Copies:
    def __init__(self, send, recv):
        self.send, self.recv, self.made = send, recv, {}

    def start(self, k, src, dst, dev):
        cp = pltpu.make_async_remote_copy(
            src_ref=src, dst_ref=dst, send_sem=self.send.at[k], recv_sem=self.recv.at[k],
            device_id=dev, device_id_type=MESH,
        )
        cp.start()
        self.made[k] = cp

    def arrived(self, *ks):
        for k in ks:
            self.made[k].wait_recv()

    def finish(self):
        for cp in self.made.values():
            cp.wait_send()


def enter(peers):
    barrier = pltpu.get_barrier_semaphore()
    for dev in peers:
        pl.semaphore_signal(barrier, inc=1, device_id=dev, device_id_type=MESH)
    pl.semaphore_wait(barrier, len(peers))


OWN, ABOVE, BELOW, FAR = 0, 2, 4, 6


class PieceGather:
    def __init__(self, buf, cps, up, down, sib, at):
        self.buf, self.cps, self.up, self.down, self.sib, self.at = buf, cps, up, down, sib, at

    def begin(self, k):
        buf, at, n = self.buf, self.at[k], len(self.at)
        self.cps.start(k, buf.at[(OWN,) + at], buf.at[(BELOW,) + at], self.up)
        self.cps.start(n + k, buf.at[(OWN,) + at], buf.at[(ABOVE,) + at], self.down)

    def middle(self, k):
        buf, at, n = self.buf, self.at[k], len(self.at)
        self.cps.arrived(k, n + k)
        if k % 2 == 0:
            self.cps.start(2 * n + k, buf.at[(BELOW,) + at], buf.at[(FAR,) + at], self.up)
        else:
            self.cps.start(2 * n + k, buf.at[(ABOVE,) + at], buf.at[(FAR,) + at], self.down)

    def share(self, slot):
        self.cps.start(3 * len(self.at) + slot // 2, self.buf.at[slot], self.buf.at[slot + 1], self.sib)

    def shared(self, *slots):
        self.cps.arrived(*(3 * len(self.at) + slot // 2 for slot in slots))

    def last(self):
        n = len(self.at)
        self.cps.arrived(*range(2 * n, 3 * n))
        self.share(FAR)


NT = (((1,), (1,)), ((), ()))
TN = (((0,), (0,)), ((), ()))


def kernel(
    hidden_t, down_h, resid, grad, gain, w_up_t, w_down, sel, sel_back,
    gh_out, gb_out, gu_out, gd_out,
    hid, down, wu, wd, rows, cots, normed,
    acc, sib_out, sib_in, z_out, z_in, x_out, x_in, pick_r, pick_c, resid_v, grad_v,
    pre, dact, act, dpre, act_t, dpre_t, v_out, v_in,
    stage, dn, sd_out, sd_in, far_out, far_in, dir_out, dir_in, sum_out, sum_in,
    drow, back_in, x2_out, x2_in, ds, fp, fin, gh_v,
    a_s, a_r, ca_s, ca_r, cg_s, cg_r, sb_s, sb_r, z_s, z_r, x_s, x_r, ra_s, ra_r, rg_s, rg_r,
    sd_s, sd_r, fr_s, fr_r, nd_s, nd_r, ns_s, ns_r, ba_s, ba_r, x2_s, x2_r, dg_s, dg_r, f_s, f_r, v_s, v_r, local_sem,
):
    where = place()
    xl, y, xh, z, c = where
    g, t = gid(xl, y), tid(xh, z, c)
    me = z * 2 + c
    head = g // 2
    width = resid.shape[1]
    model = rows.shape[2]
    inner = hid.shape[1]
    slots = rows.shape[1]
    part = inner // 2
    quarter = inner // 4

    loads = [pltpu.make_async_copy(hidden_t, hid.at[g], local_sem.at[0])]
    for i in range(2):
        tok = pl.ds(pl.multiple_of((8 * i + me) * 64, 64), 64)
        loads.append(pltpu.make_async_copy(grad.at[tok], grad_v.at[pl.ds(64 * i, 64)], local_sem.at[1 + i]))
        loads.append(pltpu.make_async_copy(resid.at[tok], resid_v.at[pl.ds(64 * i, 64)], local_sem.at[3 + i]))
    late = [
        pltpu.make_async_copy(down_h, down, local_sem.at[5]),
        pltpu.make_async_copy(w_down, wd, local_sem.at[6]),
        pltpu.make_async_copy(w_up_t, wu, local_sem.at[7]),
    ]
    for cp in loads + late[:1]:
        cp.start()

    xp = (gid(1 - xl, y), t)
    yp, ym = (gid(xl, y + 1), t), (gid(xl, y + 3), t)
    sib = (g, tid(xh, z, 1 - c))
    xhp = (g, tid(1 - xh, z, c))
    zup, zdown = (g, tid(xh, z + 1, c)), (g, tid(xh, z + 3, c))
    group_peers = [(lax.rem(g + k, GROUPS), t) for k in range(1, GROUPS)]
    z_peers = [(g, tid(xh, z + k, c)) for k in range(1, 4)]
    cross_peers = [(g, tid(xh, z + k, 1 - c)) for k in range(1, 4)]
    with jax.named_scope("enter"):
        enter(group_peers + z_peers + cross_peers + [sib, xhp])
        for cp in loads:
            cp.wait()

    a, ca, cg, sb = Copies(a_s, a_r), Copies(ca_s, ca_r), Copies(cg_s, cg_r), Copies(sb_s, sb_r)
    xx, ra, rg = Copies(x_s, x_r), Copies(ra_s, ra_r), Copies(rg_s, rg_r)
    sd, fr, nd, ns = Copies(sd_s, sd_r), Copies(fr_s, fr_r), Copies(nd_s, nd_r), Copies(ns_s, ns_r)
    ba, x2, dg, f = Copies(ba_s, ba_r), Copies(x2_s, x2_r), Copies(dg_s, dg_r), Copies(f_s, f_r)
    vx = Copies(v_s, v_r)

    low, high = pl.ds(0, part), pl.ds(part, part)

    def pass_hidden(k, shard, rows_of, to):
        piece = hid.at[shard, rows_of]
        a.start(k, piece, piece, to)

    def cols(j):
        return pl.ds(pl.multiple_of(j * width, 128), width)

    def deal(copies, picked, buf, values):
        picked[...] = jnp.dot(sel[...], values, preferred_element_type=F32).astype(BF16).reshape(picked.shape)
        for k in range(1, GROUPS):
            to = lax.rem(g + k, GROUPS)
            copies.start(k - 1, picked.at[to // 2], buf.at[OWN, :, cols(g)], (to, t))
        buf[OWN, :, cols(g)] = picked[head]

    deal(ca, pick_c, cots, grad_v[...])

    for k, rows_of, to in ((0, low, xp), (2, low, yp), (5, high, ym), (1, high, xp), (3, high, yp), (4, low, ym)):
        pass_hidden(k, g, rows_of, to)
    for cp in late[1:]:
        cp.start()

    columns = [(slice(None), cols(lax.rem(g + GROUPS - k, GROUPS))) for k in range(GROUPS)]
    cot_ring = PieceGather(cots, cg, zup, zdown, sib, columns)
    row_ring = PieceGather(rows, rg, zup, zdown, sib, columns)
    ds_ring = PieceGather(ds, dg, zup, zdown, sib, [(pl.ds(0, 64),), (pl.ds(64, 64),)])

    order = [
        (xl, y), (1 - xl, y), (xl, lax.rem(y + 3, 4)), (xl, lax.rem(y + 1, 4)), (xl, lax.rem(y + 2, 4)),
        (1 - xl, lax.rem(y + 3, 4)), (1 - xl, lax.rem(y + 1, 4)), (1 - xl, lax.rem(y + 2, 4)),
    ]

    def multiply(k):
        sx, sy = order[k]
        acc[k] = lax.dot_general(hid[gid(sx, sy)], down[...], TN, preferred_element_type=F32).reshape(2, 64, width)
        sib_out[k] = acc[k, 1 - c].astype(BF16)
        sb.start(k, sib_out.at[k], sib_in.at[k], sib)

    def z_copy(k):
        sx, sy = order[k]
        return pltpu.make_async_remote_copy(
            src_ref=z_out.at[k], dst_ref=z_in.at[sx, z], send_sem=z_s.at[k], recv_sem=z_r.at[sx, z],
            device_id=(g, tid(xh, sy, c)), device_id_type=MESH,
        )

    def pass_on(k):
        sx, sy = order[k]
        sb.arrived(k)
        z_out[k] = (acc[k, c] + sib_in[k].astype(F32)).astype(BF16)

        @pl.when(sy != z)
        def _():
            z_copy(k).start()

        @pl.when(sy == z)
        def _():
            z_in[sx, z] = z_out[k]

    k_step = 1024

    def product(total, values, weights, lo, hi):
        r = pl.ds(lo * slots, (hi - lo) * slots)
        total[r, :] = jnp.zeros(((hi - lo) * slots, total.shape[1]), F32)

        @pl.loop(0, model // k_step)
        def _(k):
            kc = pl.ds(pl.multiple_of(k * k_step, 128), k_step)
            total[r, :] += lax.dot_general(
                values[lo:hi, :, kc].reshape((hi - lo) * slots, k_step), weights[:, kc], NT,
                preferred_element_type=F32,
            )

    with jax.named_scope("gather_hidden"):
        late[0].wait()
        multiply(0)
        before, after, beside, far = gid(xl, y + 3), gid(xl, y + 1), gid(1 - xl, y), gid(xl, y + 2)
        cot_ring.begin(0)
        for k in range(1, GROUPS):
            ca.arrived(k - 1)
            cot_ring.begin(k)
        cot_ring.share(OWN)
        a.arrived(2)
        pass_hidden(6, before, low, yp)
        a.arrived(5)
        pass_hidden(7, after, high, ym)
        a.arrived(0)
        pass_hidden(8, beside, low, yp)
        pass_hidden(10, beside, low, ym)
        a.arrived(1)
        pass_hidden(9, beside, high, yp)
        pass_hidden(11, beside, high, ym)
        multiply(1)
        pass_on(0)
        a.arrived(3)
        multiply(2)
        pass_on(1)
        a.arrived(4)
        multiply(3)
        pass_on(2)
        a.arrived(6)
        pass_hidden(12, far, low, xp)
        a.arrived(7)
        pass_hidden(13, far, high, xp)
        multiply(4)
        pass_on(3)
        pass_on(4)
    with jax.named_scope("gather_cots"):
        for k in range(GROUPS):
            cot_ring.middle(k)
        cot_ring.share(BELOW)
        cot_ring.share(ABOVE)
    with jax.named_scope("gather_rest"):
        a.arrived(8, 9)
        multiply(5)
        a.arrived(10, 11)
        multiply(6)
        pass_on(5)
        pass_on(6)
        a.arrived(12, 13)
        multiply(7)
        pass_on(7)
    with jax.named_scope("sum_stream"):
        for i, sx in enumerate((xl, 1 - xl)):
            for dz in range(1, 4):
                src = lax.rem(z + dz, 4)
                pltpu.make_async_remote_copy(
                    src_ref=z_out.at[0], dst_ref=z_in.at[sx, src], send_sem=z_s.at[0], recv_sem=z_r.at[sx, src],
                    device_id=(g, tid(xh, z + dz, c)), device_id_type=MESH,
                ).wait_recv()
            parts = z_in[sx].astype(F32)
            x_out[sx] = ((parts[0] + parts[1]) + (parts[2] + parts[3])).astype(BF16)
            xx.start(i, x_out.at[sx], x_in.at[sx], xhp)
        xx.arrived(0, 1)
        total = (x_out[...].astype(F32) + x_in[...].astype(F32)).reshape(2 * 64, width)
        stream = (resid_v[...].astype(F32) + total).astype(BF16)
    with jax.named_scope("deal_rows"):
        deal(ra, pick_r, rows, stream)
        row_ring.begin(0)
        cot_ring.last()
        for k in range(1, GROUPS):
            ra.arrived(k - 1)
            row_ring.begin(k)
        row_ring.share(OWN)

    def gain_at(j):
        return gain[pl.ds(head, 1), cols(j)]

    def norm_shard(slot):
        def add(j, squares):
            v = rows[slot, :, cols(j)].astype(F32)
            return squares + v * v

        squares = lax.fori_loop(0, GROUPS, add, jnp.zeros((slots, width), F32))
        inv = lax.rsqrt(jnp.sum(squares, axis=-1, keepdims=True) * (1.0 / model) + 1e-06)

        @pl.loop(0, GROUPS)
        def _(j):
            v = rows[slot, :, cols(j)].astype(F32)
            normed[slot, :, cols(j)] = (v * inv * gain_at(j)).astype(BF16)

        return inv

    def activate(slot):
        r = pl.ds(slot * slots, slots)
        p = pre[r, :]
        s = jax.nn.sigmoid(p)
        act[r, :] = (p * s).astype(BF16)
        d = (dact[r, :] * s * (1.0 + p * (1.0 - s))).astype(BF16)
        dpre[r, :] = d
        v_out[slot] = jnp.broadcast_to(jnp.sum(d.astype(F32) * p, axis=-1, keepdims=True), v_out.shape[1:])

    with jax.named_scope("gather_rows"):
        cot_ring.shared(OWN, BELOW, ABOVE, FAR)
        late[1].wait()
        late[2].wait()
        inv_own = norm_shard(OWN)
        for k in range(GROUPS):
            row_ring.middle(k)
        row_ring.share(BELOW)
        row_ring.share(ABOVE)
        product(dact, cots, wd, 0, 8)
        row_ring.shared(OWN)
        norm_shard(OWN + 1)
        norm_shard(BELOW)
        norm_shard(ABOVE)
        row_ring.shared(BELOW)
        row_ring.shared(ABOVE)
        norm_shard(BELOW + 1)
        norm_shard(ABOVE + 1)
        row_ring.last()
        product(pre, normed, wu, 0, FAR)
        for slot in range(FAR):
            activate(slot)
        norm_shard(FAR)
        row_ring.shared(FAR)
        norm_shard(FAR + 1)

    with jax.named_scope("heads"):
        product(pre, normed, wu, FAR, 8)
        activate(FAR)
        activate(FAR + 1)
        for slot in range(1, 8):
            core = 1 - c if slot % 2 else c
            vx.start(slot - 1, v_out.at[slot], v_in.at[slot], (g, tid(xh, z + (0, 1, 3, 2)[slot // 2], core)))

    def dn_multiply(i):
        stage[...] = jnp.dot(
            dpre[...], wu[:, cols(lax.rem(g + i, GROUPS))], preferred_element_type=F32
        ).reshape(stage.shape)
        dn[i] = stage[:, 0]
        sd_out[i] = stage[:, 1].astype(BF16)
        sd.start(i, sd_out.at[i], sd_in.at[i], sib)

    def toward(i):
        return (zup, zdown, ABOVE // 2, BELOW // 2) if i % 2 == 0 else (zdown, zup, BELOW // 2, ABOVE // 2)

    def dn_split(i):
        to, other, z_to, z_other = toward(i)
        sd.arrived(i)
        dn[i] = dn[i] + sd_in[i].astype(F32)
        far_out[i] = dn[i, FAR // 2].astype(BF16)
        fr.start(i, far_out.at[i], far_in.at[i], to)
        dir_out[i] = dn[i, z_other].astype(BF16)
        nd.start(i, dir_out.at[i], dir_in.at[i], other)

    def dn_forward(i):
        to, other, z_to, z_other = toward(i)
        fr.arrived(i)
        sum_out[i] = (dn[i, z_to] + far_in[i].astype(F32)).astype(BF16)
        ns.start(i, sum_out.at[i], sum_in.at[i], to)

    def dn_finish(i):
        to = lax.rem(g + i, GROUPS)
        ns.arrived(i)
        nd.arrived(i)
        q = (dn[i, 0] + sum_in[i].astype(F32) + dir_in[i].astype(F32)) * gain_at(to)
        value = (inv_own * q - rows[OWN, :, cols(to)].astype(F32) * back).astype(BF16)
        if i == 0:
            back_in[g] = value
        else:
            drow[i] = value
            ba.start(i - 1, drow.at[i], back_in.at[g], (to, t))

    with jax.named_scope("row_gradients"):
        for i in range(GROUPS + 3):
            if i < 8:
                dn_multiply(i)
            if 0 <= i - 1 < 8:
                dn_split(i - 1)
            if 0 <= i - 3 < 8:
                dn_forward(i - 3)
        vx.arrived(*range(7))
        v = v_out[0]
        for slot in range(1, 8):
            v = v + v_in[slot]
        back = inv_own * inv_own * (v[:, :1] * (1.0 / model))

    def down_grad(j):
        wd[:, cols(j)] = jnp.dot(
            act_t[...], cots[:, :, cols(j)].reshape(ZC * slots, width), preferred_element_type=F32
        ).astype(BF16)

    def up_grad(j):
        wu[:, cols(j)] = jnp.dot(
            dpre_t[...], normed[:, :, cols(j)].reshape(ZC * slots, width), preferred_element_type=F32
        ).astype(BF16)

    with jax.named_scope("down_grads"):
        act_t[...] = act[...].T
        dpre_t[...] = dpre[...].T
        for i in range(3):
            dn_finish(i)
        pl.loop(0, GROUPS)(down_grad)
        gd_copy = pltpu.make_async_copy(wd, gd_out, local_sem.at[0])
        gd_copy.start()

    with jax.named_scope("norm_backward"):
        for i in range(3, GROUPS):
            dn_finish(i)

    with jax.named_scope("return_rows"):
        pl.loop(0, 3)(up_grad)
        ba.arrived(*range(GROUPS - 1))
        x2_out[...] = jnp.dot(
            sel_back[...], back_in[...].reshape(GROUPS * slots, width), preferred_element_type=F32
        ).astype(BF16)
        halves = (pl.ds(0, 64), pl.ds(64, 64))
        for i, h in enumerate(halves):
            x2.start(i, x2_out.at[h], x2_in.at[h], xhp)
        for i, h in enumerate(halves):
            x2.arrived(i)
            ds[OWN, h, :] = (
                grad_v[h, :].astype(F32) + (x2_out[h, :].astype(F32) + x2_in[h, :].astype(F32))
            ).astype(BF16)
            ds_ring.begin(i)
        ds_ring.share(OWN)
    with jax.named_scope("gather_dstream"):
        pl.loop(3, GROUPS)(up_grad)
        gu_copy = pltpu.make_async_copy(wu, gu_out, local_sem.at[1])
        gu_copy.start()
        ds_ring.middle(0)
        ds_ring.middle(1)
        ds_ring.share(BELOW)
        ds_ring.share(ABOVE)
        ds_ring.last()
        ds_ring.shared(OWN, BELOW, ABOVE, FAR)

    def tokens_of(sx, sy):
        ahead = lax.rem(sy + 4 - z, 4)
        slot = jnp.where(ahead == 3, BELOW, jnp.where(ahead == 2, FAR, ahead * 2))
        at = pl.ds(pl.multiple_of(sx * 64, 64), 64)
        return [ds[slot + c, at, :], ds[slot + 1 - c, at, :]]

    def hidden_grads(i, first, second, r):
        both = jnp.concatenate(tokens_of(*first) + tokens_of(*second), axis=0)
        p = lax.dot_general(down[r, :], both, NT, preferred_element_type=F32).astype(BF16)
        fp[i, r, :] = p[:, :128]
        fp[i + 1, r, :] = p[:, 128:]

    y1, y2, y3 = lax.rem(y + 1, 4), lax.rem(y + 2, 4), lax.rem(y + 3, 4)
    quarters = [pl.ds(m * quarter, quarter) for m in range(4)]

    def f_start(kind, m, src, dst, to):
        r = quarters[m]
        f.start(kind * 4 + m, fp.at[src, r], fin.at[dst, r], to)

    def f_sum(dst, m, *terms):
        r = quarters[m]
        total = fp[dst, r, :].astype(F32)
        for term in terms:
            total = total + fin[term, r, :].astype(F32)
        return total.astype(BF16)

    def f_begin(m):
        r = quarters[m]
        hidden_grads(2, (1 - xl, y1), (1 - xl, y3), r)
        f_start(0, m, 2, 0, yp)
        f_start(1, m, 3, 1, ym)
        hidden_grads(0, (1 - xl, y2), (xl, y2), r)
        f_start(2, m, 0, 2, xp)
        hidden_grads(4, (xl, y1), (xl, y3), r)
        if m % 2 == 0:
            f_start(3, m, 5, 4, ym)
        else:
            f_start(3, m, 4, 3, yp)
        hidden_grads(6, (1 - xl, y), (xl, y), r)

    def f_far(m):
        f.arrived(8 + m)
        fp[1, quarters[m], :] = f_sum(1, m, 2)
        f_start(4, m, 1, 6, yp if m % 2 == 0 else ym)

    def f_side(m):
        f.arrived(m, 4 + m)
        fp[6, quarters[m], :] = f_sum(6, m, 0, 1)
        f_start(5, m, 6, 5, xp)

    def f_near(m):
        f.arrived(16 + m)
        i = 4 if m % 2 == 0 else 5
        fp[i, quarters[m], :] = f_sum(i, m, 6)
        f_start(6, m, i, i - 1, yp if m % 2 == 0 else ym)

    def f_end(m):
        f.arrived(12 + m, 20 + m, 24 + m)
        gh_v[quarters[m], :] = f_sum(7, m, 3, 4, 5)

    def backbone_grad(m):
        r = pl.ds(pl.multiple_of(m * quarter, 16), quarter)
        total = jnp.zeros((quarter, width), F32)
        for i in range(4):
            left = jnp.concatenate([hid[2 * i, r, :], hid[2 * i + 1, r, :]], axis=1)
            right = jnp.concatenate(
                tokens_of((2 * i) // 4, (2 * i) % 4) + tokens_of((2 * i + 1) // 4, (2 * i + 1) % 4), axis=0)
            total = total + jnp.dot(left, right, preferred_element_type=F32)
        down[r, :] = total.astype(BF16)

    with jax.named_scope("hidden_grads"):
        for m in range(4):
            f_begin(m)
    with jax.named_scope("sum_hidden_grads"):
        f_far(0)
        f_far(1)
        f_side(0)
        f_far(2)
        f_far(3)
        pl.loop(0, 2)(backbone_grad)
        f_side(1)
        f_near(0)
        f_near(1)
        f_side(2)
        f_side(3)
        pl.loop(2, 4)(backbone_grad)
        gb_copy = pltpu.make_async_copy(down, gb_out, local_sem.at[2])
        gb_copy.start()
        f_near(2)
        f_near(3)
        for m in range(4):
            f_end(m)
        gh_copy = pltpu.make_async_copy(gh_v, gh_out, local_sem.at[3])
        gh_copy.start()

    with jax.named_scope("finish"):
        for cps in (a, ca, cg, sb, xx, ra, rg, sd, fr, nd, ns, ba, x2, dg, f, vx):
            cps.finish()
        for k in range(GROUPS):
            @pl.when(order[k][1] != z)
            def _():
                z_copy(k).wait_send()
        for cp in (gd_copy, gu_copy, gb_copy, gh_copy):
            cp.wait()


def run(hidden_t, down, resid, grad, gain, w_up_t, w_down, sel, sel_back):
    inner, tokens = hidden_t.shape
    width = down.shape[1]
    slots = sel.shape[0] // 4
    model = width * GROUPS
    units = w_down.shape[0]
    any_spec = pl.BlockSpec(memory_space=pl.ANY)
    vmem = pl.BlockSpec(memory_space=pltpu.VMEM)
    dma = pltpu.SemaphoreType.DMA
    sems = []
    for n in ((14,), (7,), (28,), (8,)):
        sems += [dma(n), dma(n)]
    sems += [dma((8,)), dma((2, 4))]
    for n in ((2,), (7,), (28,), (8,), (8,), (8,), (8,), (7,), (2,), (10,), (28,), (7,)):
        sems += [dma(n), dma(n)]
    sems += [dma((8,))]
    piece = (64, width)
    return pl.pallas_call(
        kernel,
        out_shape=(
            jax.ShapeDtypeStruct((inner, tokens), BF16),
            jax.ShapeDtypeStruct((inner, width), BF16),
            jax.ShapeDtypeStruct((units, model), BF16),
            jax.ShapeDtypeStruct((units, model), BF16),
        ),
        in_specs=[any_spec] * 4 + [vmem] + [any_spec] * 2 + [vmem] * 2,
        out_specs=(any_spec,) * 4,
        scratch_shapes=[
            pltpu.VMEM((GROUPS, inner, tokens), BF16),
            pltpu.VMEM((inner, width), BF16),
            pltpu.VMEM((units, model), BF16),
            pltpu.VMEM((units, model), BF16),
            pltpu.VMEM((ZC, slots, model), BF16),
            pltpu.VMEM((ZC, slots, model), BF16),
            pltpu.VMEM((ZC, slots, model), BF16),
            pltpu.VMEM((8, 2) + piece, F32),
            pltpu.VMEM((8,) + piece, BF16),
            pltpu.VMEM((8,) + piece, BF16),
            pltpu.VMEM((8,) + piece, BF16),
            pltpu.VMEM((2, 4) + piece, BF16),
            pltpu.VMEM((2,) + piece, BF16),
            pltpu.VMEM((2,) + piece, BF16),
            pltpu.VMEM((4, slots, width), BF16),
            pltpu.VMEM((4, slots, width), BF16),
            pltpu.VMEM((128, width), BF16),
            pltpu.VMEM((128, width), BF16),
            pltpu.VMEM((ZC * slots, units), F32),
            pltpu.VMEM((ZC * slots, units), F32),
            pltpu.VMEM((ZC * slots, units), BF16),
            pltpu.VMEM((ZC * slots, units), BF16),
            pltpu.VMEM((units, ZC * slots), BF16),
            pltpu.VMEM((units, ZC * slots), BF16),
            pltpu.VMEM((ZC, slots, 128), F32),
            pltpu.VMEM((ZC, slots, 128), F32),
            pltpu.VMEM((4, 2, slots, width), F32),
            pltpu.VMEM((8, 4, slots, width), F32),
            pltpu.VMEM((8, 4, slots, width), BF16),
            pltpu.VMEM((8, 4, slots, width), BF16),
        ]
        + [pltpu.VMEM((8, slots, width), BF16)] * 6
        + [
            pltpu.VMEM((8, slots, width), BF16),
            pltpu.VMEM((8, slots, width), BF16),
            pltpu.VMEM((128, width), BF16),
            pltpu.VMEM((128, width), BF16),
            pltpu.VMEM((8, 128, width), BF16),
            pltpu.VMEM((8, inner, tokens), BF16),
            pltpu.VMEM((7, inner, tokens), BF16),
            pltpu.VMEM((inner, tokens), BF16),
        ]
        + sems,
        compiler_params=pltpu.CompilerParams(
            collective_id=0, has_side_effects=True, vmem_limit_bytes=62 * 1024 * 1024
        ),
        name="backbone_and_heads",
    )(hidden_t, down, resid, grad, gain, w_up_t, w_down, sel, sel_back)


def copy_kernel(*refs):
    n = (len(refs) - 2) // 3
    held, sem_in, sem_out = refs[2 * n : 3 * n], refs[-2], refs[-1]
    copies = []
    for src, mid, dst in zip(refs[:n], held, refs[n : 2 * n]):
        step = src.shape[0] // 3
        for r in range(0, src.shape[0], step):
            rows_of, k = pl.ds(r, step), len(copies)
            copies.append((
                pltpu.make_async_copy(src.at[rows_of], mid.at[rows_of], sem_in.at[k]),
                pltpu.make_async_copy(mid.at[rows_of], dst.at[rows_of], sem_out.at[k]),
            ))
    for fetch, _ in copies:
        fetch.start()
    for fetch, store in copies:
        fetch.wait()
        store.start()
    for _, store in copies:
        store.wait()


def place_results(*arrays):
    any_spec = pl.BlockSpec(memory_space=pl.ANY)
    count = 3 * len(arrays)
    return pl.pallas_call(
        copy_kernel,
        out_shape=tuple(jax.ShapeDtypeStruct(a.shape, a.dtype) for a in arrays),
        in_specs=[any_spec] * len(arrays),
        out_specs=(any_spec,) * len(arrays),
        scratch_shapes=[pltpu.VMEM(a.shape, a.dtype) for a in arrays]
        + [pltpu.SemaphoreType.DMA((count,)), pltpu.SemaphoreType.DMA((count,))],
        compiler_params=pltpu.CompilerParams(vmem_limit_bytes=62 * 1024 * 1024),
        name="place_results",
    )(*arrays)


def local(backbone_hidden, backbone_down, residual, head_grad, gain, w_up, w_down, route):
    groups = lax.axis_size("group")
    heads = gain.shape[0]
    zc = lax.rem(lax.axis_index("tensor"), ZC)
    blocks, _, slot_count = route.shape
    block_len = residual.shape[0] // blocks
    own = lax.dynamic_index_in_dim(route.reshape(2, ZC, heads, slot_count), zc, 1, keepdims=False)
    wanted = jnp.where(own >= 0, own + (jnp.arange(2, dtype=jnp.int32) * block_len)[:, None, None], -1)
    wanted = wanted.transpose(1, 0, 2).reshape(heads, 2 * slot_count)
    positions = jnp.arange(2 * block_len, dtype=jnp.int32)
    sel = (wanted.reshape(-1)[:, None] == positions[None]).astype(BF16)
    twice = jnp.repeat(wanted, groups // heads, axis=0).reshape(-1)
    sel_back = (positions[:, None] == twice[None]).astype(BF16)
    gh, gb, gu, gd = run(
        backbone_hidden.T, backbone_down, residual, head_grad, gain, w_up.T, w_down, sel, sel_back
    )
    gh, gb, gu, gd = place_results(gh, gb, gu, gd)
    return (gh.T, gb, gu.T, gd)


def solution(mesh):
    placed = (
        P("group", "tensor"),
        P("tensor", "group"),
        P(None, "group"),
        P(None, "group"),
        P(),
        P(None, ("group", "tensor")),
        P(("group", "tensor"), None),
        P(),
    )
    return jax.shard_map(
        local,
        mesh=mesh,
        in_specs=placed,
        out_specs=(
            P("group", "tensor"),
            P("tensor", "group"),
            P(None, ("group", "tensor")),
            P(("group", "tensor"), None),
        ),
        check_vma=False,
    )
```

```python
import jax
import jax.numpy as jnp
from jax import lax
from jax.experimental import pallas as pl
from jax.experimental.pallas import tpu as pltpu
from jax.sharding import PartitionSpec as P

MESH = pl.DeviceIdType.MESH
F32 = jnp.float32
BF16 = jnp.bfloat16
GROUPS = 8
ZC = 8


def place():
    g = lax.axis_index("group")
    t = lax.axis_index("tensor")
    return g // 4, g % 4, t // 8, (t // 2) % 4, t % 2


def gid(xl, y):
    return xl * 4 + lax.rem(y, 4)


def tid(xh, z, c):
    return xh * 8 + lax.rem(z, 4) * 2 + c


class Copies:
    def __init__(self, send, recv):
        self.send, self.recv, self.made = send, recv, {}

    def start(self, k, src, dst, dev):
        cp = pltpu.make_async_remote_copy(
            src_ref=src, dst_ref=dst, send_sem=self.send.at[k], recv_sem=self.recv.at[k],
            device_id=dev, device_id_type=MESH,
        )
        cp.start()
        self.made[k] = cp

    def arrived(self, *ks):
        for k in ks:
            self.made[k].wait_recv()

    def finish(self):
        for cp in self.made.values():
            cp.wait_send()


def enter(peers):
    barrier = pltpu.get_barrier_semaphore()
    for dev in peers:
        pl.semaphore_signal(barrier, inc=1, device_id=dev, device_id_type=MESH)
    pl.semaphore_wait(barrier, len(peers))


OWN, ABOVE, BELOW, FAR = 0, 2, 4, 6


class PieceGather:
    def __init__(self, buf, cps, up, down, sib, at):
        self.buf, self.cps, self.up, self.down, self.sib, self.at = buf, cps, up, down, sib, at

    def begin(self, k):
        buf, at, n = self.buf, self.at[k], len(self.at)
        self.cps.start(k, buf.at[(OWN,) + at], buf.at[(BELOW,) + at], self.up)
        self.cps.start(n + k, buf.at[(OWN,) + at], buf.at[(ABOVE,) + at], self.down)

    def middle(self, k):
        buf, at, n = self.buf, self.at[k], len(self.at)
        self.cps.arrived(k, n + k)
        if k % 2 == 0:
            self.cps.start(2 * n + k, buf.at[(BELOW,) + at], buf.at[(FAR,) + at], self.up)
        else:
            self.cps.start(2 * n + k, buf.at[(ABOVE,) + at], buf.at[(FAR,) + at], self.down)

    def share(self, slot):
        self.cps.start(3 * len(self.at) + slot // 2, self.buf.at[slot], self.buf.at[slot + 1], self.sib)

    def shared(self, *slots):
        self.cps.arrived(*(3 * len(self.at) + slot // 2 for slot in slots))

    def last(self):
        n = len(self.at)
        self.cps.arrived(*range(2 * n, 3 * n))
        self.share(FAR)


NT = (((1,), (1,)), ((), ()))
TN = (((0,), (0,)), ((), ()))


def kernel(
    hidden_t, down_h, resid, grad, gain_h, w_up_t, w_down, places,
    gh_v, down, wu, wd,
    hid, gain, sel_of, rows, cots, normed,
    acc, sib_out, sib_in, z_out, z_in, x_out, x_in, pick_r, pick_c, resid_v, grad_v,
    pre, dact, act, dpre, act_t, dpre_t, v_out, v_in,
    stage, dn, sd_out, sd_in, far_out, far_in, dir_out, dir_in, sum_out, sum_in,
    drow, back_in, x2_out, x2_in, ds, fp, fin,
    a_s, a_r, ca_s, ca_r, cg_s, cg_r, sb_s, sb_r, z_s, z_r, x_s, x_r, ra_s, ra_r, rg_s, rg_r,
    sd_s, sd_r, fr_s, fr_r, nd_s, nd_r, ns_s, ns_r, ba_s, ba_r, x2_s, x2_r, dg_s, dg_r, f_s, f_r, v_s, v_r, local_sem,
):
    where = place()
    xl, y, xh, z, c = where
    g, t = gid(xl, y), tid(xh, z, c)
    me = z * 2 + c
    head = g // 2
    width = resid.shape[1]
    model = rows.shape[2]
    inner = hid.shape[1]
    slots = rows.shape[1]
    part = inner // 2
    quarter = inner // 4

    loads = [pltpu.make_async_copy(hidden_t, hid.at[g], local_sem.at[0])]
    for i in range(2):
        tok = pl.ds(pl.multiple_of((8 * i + me) * 64, 64), 64)
        loads.append(pltpu.make_async_copy(grad.at[tok], grad_v.at[pl.ds(64 * i, 64)], local_sem.at[1 + i]))
        loads.append(pltpu.make_async_copy(resid.at[tok], resid_v.at[pl.ds(64 * i, 64)], local_sem.at[3 + i]))
    loads.append(pltpu.make_async_copy(places, sel_of, local_sem.at[8]))
    loads.append(pltpu.make_async_copy(gain_h, gain, local_sem.at[9]))
    late = [
        pltpu.make_async_copy(down_h, down, local_sem.at[5]),
        pltpu.make_async_copy(w_down, wd, local_sem.at[6]),
        pltpu.make_async_copy(w_up_t, wu, local_sem.at[7]),
    ]
    for cp in loads + late[:1]:
        cp.start()

    xp = (gid(1 - xl, y), t)
    yp, ym = (gid(xl, y + 1), t), (gid(xl, y + 3), t)
    sib = (g, tid(xh, z, 1 - c))
    xhp = (g, tid(1 - xh, z, c))
    zup, zdown = (g, tid(xh, z + 1, c)), (g, tid(xh, z + 3, c))
    group_peers = [(lax.rem(g + k, GROUPS), t) for k in range(1, GROUPS)]
    z_peers = [(g, tid(xh, z + k, c)) for k in range(1, 4)]
    cross_peers = [(g, tid(xh, z + k, 1 - c)) for k in range(1, 4)]
    with jax.named_scope("enter"):
        enter(group_peers + z_peers + cross_peers + [sib, xhp])
        for cp in loads:
            cp.wait()

    a, ca, cg, sb = Copies(a_s, a_r), Copies(ca_s, ca_r), Copies(cg_s, cg_r), Copies(sb_s, sb_r)
    xx, ra, rg = Copies(x_s, x_r), Copies(ra_s, ra_r), Copies(rg_s, rg_r)
    sd, fr, nd, ns = Copies(sd_s, sd_r), Copies(fr_s, fr_r), Copies(nd_s, nd_r), Copies(ns_s, ns_r)
    ba, x2, dg, f = Copies(ba_s, ba_r), Copies(x2_s, x2_r), Copies(dg_s, dg_r), Copies(f_s, f_r)
    vx = Copies(v_s, v_r)

    low, high = pl.ds(0, part), pl.ds(part, part)

    def pass_hidden(k, shard, rows_of, to):
        piece = hid.at[shard, rows_of]
        a.start(k, piece, piece, to)

    def cols(j):
        return pl.ds(pl.multiple_of(j * width, 128), width)

    def select():
        lane = lax.broadcasted_iota(jnp.int32, (128, 4 * slots), 1)
        token = lax.broadcasted_iota(jnp.int32, (128, 4 * slots), 0)
        second = lax.rem(lane, slots) >= slots // 2
        places = [sel_of[8 * i + me, h : h + 1, :] for h in range(4) for i in range(2)]
        wanted = jnp.broadcast_to(jnp.concatenate(places, axis=1), lane.shape)
        hit = (wanted >= 0) & (wanted + jnp.where(second, 64, 0) == token)
        return jnp.where(hit, 1.0, 0.0).astype(BF16)

    def deal(copies, picked, buf, values):
        chosen = lax.dot_general(select(), values, TN, preferred_element_type=F32)
        picked[...] = chosen.astype(BF16).reshape(picked.shape)
        for k in range(1, GROUPS):
            to = lax.rem(g + k, GROUPS)
            copies.start(k - 1, picked.at[to // 2], buf.at[OWN, :, cols(g)], (to, t))
        buf[OWN, :, cols(g)] = picked[head]

    deal(ca, pick_c, cots, grad_v[...])

    for k, rows_of, to in ((0, low, xp), (2, low, yp), (5, high, ym), (1, high, xp), (3, high, yp), (4, low, ym)):
        pass_hidden(k, g, rows_of, to)
    for cp in late[1:]:
        cp.start()

    columns = [(slice(None), cols(lax.rem(g + GROUPS - k, GROUPS))) for k in range(GROUPS)]
    cot_ring = PieceGather(cots, cg, zup, zdown, sib, columns)
    row_ring = PieceGather(rows, rg, zup, zdown, sib, columns)
    ds_ring = PieceGather(ds, dg, zup, zdown, sib, [(pl.ds(0, 64),), (pl.ds(64, 64),)])

    order = [
        (xl, y), (1 - xl, y), (xl, lax.rem(y + 3, 4)), (xl, lax.rem(y + 1, 4)), (xl, lax.rem(y + 2, 4)),
        (1 - xl, lax.rem(y + 3, 4)), (1 - xl, lax.rem(y + 1, 4)), (1 - xl, lax.rem(y + 2, 4)),
    ]

    def multiply(k):
        sx, sy = order[k]
        acc[k] = lax.dot_general(hid[gid(sx, sy)], down[...], TN, preferred_element_type=F32).reshape(2, 64, width)
        sib_out[k] = acc[k, 1 - c].astype(BF16)
        sb.start(k, sib_out.at[k], sib_in.at[k], sib)

    def z_copy(k):
        sx, sy = order[k]
        return pltpu.make_async_remote_copy(
            src_ref=z_out.at[k], dst_ref=z_in.at[sx, z], send_sem=z_s.at[k], recv_sem=z_r.at[sx, z],
            device_id=(g, tid(xh, sy, c)), device_id_type=MESH,
        )

    def pass_on(k):
        sx, sy = order[k]
        sb.arrived(k)
        z_out[k] = (acc[k, c] + sib_in[k].astype(F32)).astype(BF16)

        @pl.when(sy != z)
        def _():
            z_copy(k).start()

        @pl.when(sy == z)
        def _():
            z_in[sx, z] = z_out[k]

    k_step = 1024

    def product(total, values, weights, lo, hi):
        r = pl.ds(lo * slots, (hi - lo) * slots)
        total[r, :] = jnp.zeros(((hi - lo) * slots, total.shape[1]), F32)

        @pl.loop(0, model // k_step)
        def _(k):
            kc = pl.ds(pl.multiple_of(k * k_step, 128), k_step)
            total[r, :] += lax.dot_general(
                values[lo:hi, :, kc].reshape((hi - lo) * slots, k_step), weights[:, kc], NT,
                preferred_element_type=F32,
            )

    with jax.named_scope("gather_hidden"):
        late[0].wait()
        multiply(0)
        before, after, beside, far = gid(xl, y + 3), gid(xl, y + 1), gid(1 - xl, y), gid(xl, y + 2)
        cot_ring.begin(0)
        for k in range(1, GROUPS):
            ca.arrived(k - 1)
            cot_ring.begin(k)
        cot_ring.share(OWN)
        a.arrived(2)
        pass_hidden(6, before, low, yp)
        a.arrived(5)
        pass_hidden(7, after, high, ym)
        a.arrived(0)
        pass_hidden(8, beside, low, yp)
        pass_hidden(10, beside, low, ym)
        a.arrived(1)
        pass_hidden(9, beside, high, yp)
        pass_hidden(11, beside, high, ym)
        multiply(1)
        pass_on(0)
        a.arrived(3)
        multiply(2)
        pass_on(1)
        a.arrived(4)
        multiply(3)
        pass_on(2)
        a.arrived(6)
        pass_hidden(12, far, low, xp)
        a.arrived(7)
        pass_hidden(13, far, high, xp)
        multiply(4)
        pass_on(3)
        pass_on(4)
    with jax.named_scope("gather_cots"):
        for k in range(GROUPS):
            cot_ring.middle(k)
        cot_ring.share(BELOW)
        cot_ring.share(ABOVE)
    with jax.named_scope("gather_rest"):
        a.arrived(8, 9)
        multiply(5)
        a.arrived(10, 11)
        multiply(6)
        pass_on(5)
        pass_on(6)
        a.arrived(12, 13)
        multiply(7)
        pass_on(7)
    with jax.named_scope("sum_stream"):
        for i, sx in enumerate((xl, 1 - xl)):
            for dz in range(1, 4):
                src = lax.rem(z + dz, 4)
                pltpu.make_async_remote_copy(
                    src_ref=z_out.at[0], dst_ref=z_in.at[sx, src], send_sem=z_s.at[0], recv_sem=z_r.at[sx, src],
                    device_id=(g, tid(xh, z + dz, c)), device_id_type=MESH,
                ).wait_recv()
            parts = z_in[sx].astype(F32)
            x_out[sx] = ((parts[0] + parts[1]) + (parts[2] + parts[3])).astype(BF16)
            xx.start(i, x_out.at[sx], x_in.at[sx], xhp)
        xx.arrived(0, 1)
        total = (x_out[...].astype(F32) + x_in[...].astype(F32)).reshape(2 * 64, width)
        stream = (resid_v[...].astype(F32) + total).astype(BF16)
    with jax.named_scope("deal_rows"):
        deal(ra, pick_r, rows, stream)
        row_ring.begin(0)
        cot_ring.last()
        for k in range(1, GROUPS):
            ra.arrived(k - 1)
            row_ring.begin(k)
        row_ring.share(OWN)

    def gain_at(j):
        return gain[pl.ds(head, 1), cols(j)]

    def norm_shard(slot):
        def add(j, squares):
            v = rows[slot, :, cols(j)].astype(F32)
            return squares + v * v

        squares = lax.fori_loop(0, GROUPS, add, jnp.zeros((slots, width), F32))
        inv = lax.rsqrt(jnp.sum(squares, axis=-1, keepdims=True) * (1.0 / model) + 1e-06)

        @pl.loop(0, GROUPS)
        def _(j):
            v = rows[slot, :, cols(j)].astype(F32)
            normed[slot, :, cols(j)] = (v * inv * gain_at(j)).astype(BF16)

        return inv

    def activate(slot):
        r = pl.ds(slot * slots, slots)
        p = pre[r, :]
        s = jax.nn.sigmoid(p)
        act[r, :] = (p * s).astype(BF16)
        d = (dact[r, :] * s * (1.0 + p * (1.0 - s))).astype(BF16)
        dpre[r, :] = d
        v_out[slot] = jnp.broadcast_to(jnp.sum(d.astype(F32) * p, axis=-1, keepdims=True), v_out.shape[1:])

    with jax.named_scope("gather_rows"):
        cot_ring.shared(OWN, BELOW, ABOVE, FAR)
        late[1].wait()
        late[2].wait()
        inv_own = norm_shard(OWN)
        product(dact, cots, wd, 0, 8)
        for k in range(GROUPS):
            row_ring.middle(k)
        row_ring.share(BELOW)
        row_ring.share(ABOVE)
        row_ring.shared(OWN)
        norm_shard(OWN + 1)
        norm_shard(BELOW)
        norm_shard(ABOVE)
        row_ring.shared(BELOW)
        row_ring.shared(ABOVE)
        norm_shard(BELOW + 1)
        norm_shard(ABOVE + 1)
        row_ring.last()
        product(pre, normed, wu, 0, FAR)
        for slot in range(FAR):
            activate(slot)
        norm_shard(FAR)
        row_ring.shared(FAR)
        norm_shard(FAR + 1)

    with jax.named_scope("heads"):
        product(pre, normed, wu, FAR, 8)
        activate(FAR)
        activate(FAR + 1)
        for slot in range(1, 8):
            core = 1 - c if slot % 2 else c
            vx.start(slot - 1, v_out.at[slot], v_in.at[slot], (g, tid(xh, z + (0, 1, 3, 2)[slot // 2], core)))

    def dn_multiply(i):
        stage[...] = jnp.dot(
            dpre[...], wu[:, cols(lax.rem(g + i, GROUPS))], preferred_element_type=F32
        ).reshape(stage.shape)
        dn[i] = stage[:, 0]
        sd_out[i] = stage[:, 1].astype(BF16)
        sd.start(i, sd_out.at[i], sd_in.at[i], sib)

    def toward(i):
        return (zup, zdown, ABOVE // 2, BELOW // 2) if i % 2 == 0 else (zdown, zup, BELOW // 2, ABOVE // 2)

    def dn_split(i):
        to, other, z_to, z_other = toward(i)
        sd.arrived(i)
        dn[i] = dn[i] + sd_in[i].astype(F32)
        far_out[i] = dn[i, FAR // 2].astype(BF16)
        fr.start(i, far_out.at[i], far_in.at[i], to)
        dir_out[i] = dn[i, z_other].astype(BF16)
        nd.start(i, dir_out.at[i], dir_in.at[i], other)

    def dn_forward(i):
        to, other, z_to, z_other = toward(i)
        fr.arrived(i)
        sum_out[i] = (dn[i, z_to] + far_in[i].astype(F32)).astype(BF16)
        ns.start(i, sum_out.at[i], sum_in.at[i], to)

    def dn_finish(i):
        to = lax.rem(g + i, GROUPS)
        ns.arrived(i)
        nd.arrived(i)
        q = (dn[i, 0] + sum_in[i].astype(F32) + dir_in[i].astype(F32)) * gain_at(to)
        value = (inv_own * q - rows[OWN, :, cols(to)].astype(F32) * back).astype(BF16)
        if i == 0:
            back_in[lax.rem(g, 2), head] = value
        else:
            drow[i] = value
            ba.start(i - 1, drow.at[i], back_in.at[lax.rem(g, 2), head], (to, t))

    with jax.named_scope("row_gradients"):
        for i in range(GROUPS + 3):
            if i < 8:
                dn_multiply(i)
            if 0 <= i - 1 < 8:
                dn_split(i - 1)
            if 0 <= i - 3 < 8:
                dn_forward(i - 3)
        vx.arrived(*range(7))
        v = v_out[0]
        for slot in range(1, 8):
            v = v + v_in[slot]
        back = inv_own * inv_own * (v[:, :1] * (1.0 / model))

    def down_grad(j):
        wd[:, cols(j)] = jnp.dot(
            act_t[...], cots[:, :, cols(j)].reshape(ZC * slots, width), preferred_element_type=F32
        ).astype(BF16)

    def up_grad(j):
        wu[:, cols(j)] = jnp.dot(
            dpre_t[...], normed[:, :, cols(j)].reshape(ZC * slots, width), preferred_element_type=F32
        ).astype(BF16)

    with jax.named_scope("down_grads"):
        act_t[...] = act[...].T
        dpre_t[...] = dpre[...].T
    with jax.named_scope("norm_backward"):
        for i in range(GROUPS):
            dn_finish(i)

    with jax.named_scope("return_rows"):
        pl.loop(0, 4)(down_grad)
        ba.arrived(*range(GROUPS - 1))
        chosen = select()
        x2_out[...] = (
            jnp.dot(chosen, back_in[0].reshape(4 * slots, width), preferred_element_type=F32)
            + jnp.dot(chosen, back_in[1].reshape(4 * slots, width), preferred_element_type=F32)
        ).astype(BF16)
        halves = (pl.ds(0, 64), pl.ds(64, 64))
        for i, h in enumerate(halves):
            x2.start(i, x2_out.at[h], x2_in.at[h], xhp)
        pl.loop(4, GROUPS)(down_grad)
        pl.loop(0, 3)(up_grad)
        for i, h in enumerate(halves):
            x2.arrived(i)
            ds[OWN, h, :] = (
                grad_v[h, :].astype(F32) + (x2_out[h, :].astype(F32) + x2_in[h, :].astype(F32))
            ).astype(BF16)
            ds_ring.begin(i)
        ds_ring.share(OWN)
    with jax.named_scope("gather_dstream"):
        pl.loop(3, 6)(up_grad)
        ds_ring.middle(0)
        ds_ring.middle(1)
        ds_ring.share(BELOW)
        ds_ring.share(ABOVE)
        ds_ring.last()
        ds_ring.shared(OWN, BELOW, ABOVE, FAR)

    def tokens_of(sx, sy):
        ahead = lax.rem(sy + 4 - z, 4)
        slot = jnp.where(ahead == 3, BELOW, jnp.where(ahead == 2, FAR, ahead * 2))
        at = pl.ds(pl.multiple_of(sx * 64, 64), 64)
        return [ds[slot + c, at, :], ds[slot + 1 - c, at, :]]

    def hidden_grads(i, first, second, r):
        both = jnp.concatenate(tokens_of(*first) + tokens_of(*second), axis=0)
        p = lax.dot_general(down[r, :], both, NT, preferred_element_type=F32).astype(BF16)
        fp[i, r, :] = p[:, :128]
        fp[i + 1, r, :] = p[:, 128:]

    y1, y2, y3 = lax.rem(y + 1, 4), lax.rem(y + 2, 4), lax.rem(y + 3, 4)
    quarters = [pl.ds(m * quarter, quarter) for m in range(4)]

    def f_start(kind, m, src, dst, to):
        r = quarters[m]
        f.start(kind * 4 + m, fp.at[src, r], fin.at[dst, r], to)

    def f_sum(dst, m, *terms):
        r = quarters[m]
        total = fp[dst, r, :].astype(F32)
        for term in terms:
            total = total + fin[term, r, :].astype(F32)
        return total.astype(BF16)

    def f_begin(m):
        r = quarters[m]
        hidden_grads(2, (1 - xl, y1), (1 - xl, y3), r)
        f_start(0, m, 2, 0, yp)
        f_start(1, m, 3, 1, ym)
        hidden_grads(0, (1 - xl, y2), (xl, y2), r)
        f_start(2, m, 0, 2, xp)
        hidden_grads(4, (xl, y1), (xl, y3), r)
        hidden_grads(6, (1 - xl, y), (xl, y), r)

    def f_far(m):
        f.arrived(8 + m)
        fp[1, quarters[m], :] = f_sum(1, m, 2)
        f_start(4, m, 1, 6, yp if m % 2 == 0 else ym)

    def f_direct(m):
        if m % 2 == 0:
            f_start(3, m, 5, 4, ym)
        else:
            f_start(3, m, 4, 3, yp)

    def f_side(m):
        f.arrived(m, 4 + m)
        fp[6, quarters[m], :] = f_sum(6, m, 0, 1)
        f_start(5, m, 6, 5, xp)

    def f_near(m):
        f.arrived(16 + m)
        i = 4 if m % 2 == 0 else 5
        fp[i, quarters[m], :] = f_sum(i, m, 6)
        f_start(6, m, i, i - 1, yp if m % 2 == 0 else ym)

    def f_end(m):
        f.arrived(12 + m, 20 + m, 24 + m)
        gh_v[quarters[m], :] = f_sum(7, m, 3, 4, 5)

    def backbone_grad(m):
        r = pl.ds(pl.multiple_of(m * quarter, 16), quarter)
        total = jnp.zeros((quarter, width), F32)
        for i in range(4):
            left = jnp.concatenate([hid[2 * i, r, :], hid[2 * i + 1, r, :]], axis=1)
            right = jnp.concatenate(
                tokens_of((2 * i) // 4, (2 * i) % 4) + tokens_of((2 * i + 1) // 4, (2 * i + 1) % 4), axis=0)
            total = total + jnp.dot(left, right, preferred_element_type=F32)
        down[r, :] = total.astype(BF16)

    with jax.named_scope("hidden_grads"):
        for m in range(4):
            f_begin(m)
    with jax.named_scope("sum_hidden_grads"):
        for m in range(4):
            f_far(m)
        for m in range(4):
            f_direct(m)
        f_side(0)
        pl.loop(6, 8)(up_grad)
        pl.loop(0, 2)(backbone_grad)
        f_side(1)
        f_near(0)
        f_near(1)
        f_side(2)
        f_side(3)
        pl.loop(2, 4)(backbone_grad)
        f_near(2)
        f_near(3)
        for m in range(4):
            f_end(m)

    with jax.named_scope("finish"):
        for cps in (a, ca, cg, sb, xx, ra, rg, sd, fr, nd, ns, ba, x2, dg, f, vx):
            cps.finish()
        for k in range(GROUPS):
            @pl.when(order[k][1] != z)
            def _():
                z_copy(k).wait_send()


def run(hidden_t, down, resid, grad, gain, w_up_t, w_down, places):
    inner, tokens = hidden_t.shape
    width = down.shape[1]
    slots = 2 * places.shape[2]
    model = width * GROUPS
    units = w_down.shape[0]
    any_spec = pl.BlockSpec(memory_space=pl.ANY)
    vmem = pl.BlockSpec(memory_space=pltpu.VMEM)
    dma = pltpu.SemaphoreType.DMA
    sems = []
    for n in ((14,), (7,), (28,), (8,)):
        sems += [dma(n), dma(n)]
    sems += [dma((8,)), dma((2, 4))]
    for n in ((2,), (7,), (28,), (8,), (8,), (8,), (8,), (7,), (2,), (10,), (28,), (7,)):
        sems += [dma(n), dma(n)]
    sems += [dma((10,))]
    piece = (64, width)
    return pl.pallas_call(
        kernel,
        out_shape=(
            pltpu.VMEM((inner, tokens), BF16),
            pltpu.VMEM((inner, width), BF16),
            pltpu.VMEM((units, model), BF16),
            pltpu.VMEM((units, model), BF16),
        ),
        in_specs=[any_spec] * 8,
        out_specs=(vmem,) * 4,
        scratch_shapes=[
            pltpu.VMEM((GROUPS, inner, tokens), BF16),
            pltpu.VMEM((4, model), F32),
            pltpu.VMEM(places.shape, jnp.int32),
            pltpu.VMEM((ZC, slots, model), BF16),
            pltpu.VMEM((ZC, slots, model), BF16),
            pltpu.VMEM((ZC, slots, model), BF16),
            pltpu.VMEM((8, 2) + piece, F32),
            pltpu.VMEM((8,) + piece, BF16),
            pltpu.VMEM((8,) + piece, BF16),
            pltpu.VMEM((8,) + piece, BF16),
            pltpu.VMEM((2, 4) + piece, BF16),
            pltpu.VMEM((2,) + piece, BF16),
            pltpu.VMEM((2,) + piece, BF16),
            pltpu.VMEM((4, slots, width), BF16),
            pltpu.VMEM((4, slots, width), BF16),
            pltpu.VMEM((128, width), BF16),
            pltpu.VMEM((128, width), BF16),
            pltpu.VMEM((ZC * slots, units), F32),
            pltpu.VMEM((ZC * slots, units), F32),
            pltpu.VMEM((ZC * slots, units), BF16),
            pltpu.VMEM((ZC * slots, units), BF16),
            pltpu.VMEM((units, ZC * slots), BF16),
            pltpu.VMEM((units, ZC * slots), BF16),
            pltpu.VMEM((ZC, slots, 128), F32),
            pltpu.VMEM((ZC, slots, 128), F32),
            pltpu.VMEM((4, 2, slots, width), F32),
            pltpu.VMEM((8, 4, slots, width), F32),
            pltpu.VMEM((8, 4, slots, width), BF16),
            pltpu.VMEM((8, 4, slots, width), BF16),
        ]
        + [pltpu.VMEM((8, slots, width), BF16)] * 6
        + [
            pltpu.VMEM((8, slots, width), BF16),
            pltpu.VMEM((2, 4, slots, width), BF16),
            pltpu.VMEM((128, width), BF16),
            pltpu.VMEM((128, width), BF16),
            pltpu.VMEM((8, 128, width), BF16),
            pltpu.VMEM((8, inner, tokens), BF16),
            pltpu.VMEM((7, inner, tokens), BF16),
        ]
        + sems,
        compiler_params=pltpu.CompilerParams(
            collective_id=0, has_side_effects=True, vmem_limit_bytes=50 * 1024 * 1024
        ),
        name="backbone_and_heads",
    )(hidden_t, down, resid, grad, gain, w_up_t, w_down, places)


def copy_kernel(*refs):
    n = (len(refs) - 1) // 2
    copies = []
    for src, dst in zip(refs[:n], refs[n : 2 * n]):
        step = src.shape[0] // 3
        for r in range(0, src.shape[0], step):
            rows_of = pl.ds(r, step)
            copies.append(pltpu.make_async_copy(src.at[rows_of], dst.at[rows_of], refs[-1].at[len(copies)]))
    for cp in copies:
        cp.start()
    for cp in copies:
        cp.wait()


def place_results(*arrays):
    return pl.pallas_call(
        copy_kernel,
        out_shape=tuple(jax.ShapeDtypeStruct(a.shape, a.dtype) for a in arrays),
        in_specs=[pl.BlockSpec(memory_space=pltpu.VMEM)] * len(arrays),
        out_specs=(pl.BlockSpec(memory_space=pl.ANY),) * len(arrays),
        scratch_shapes=[pltpu.SemaphoreType.DMA((3 * len(arrays),))],
        compiler_params=pltpu.CompilerParams(vmem_limit_bytes=4 * 1024 * 1024),
        name="place_results",
    )(*arrays)


def local(backbone_hidden, backbone_down, residual, head_grad, gain, w_up, w_down, route):
    gh, gb, gu, gd = run(
        backbone_hidden.T, backbone_down, residual, head_grad, gain, w_up.T, w_down, route
    )
    gh, gb, gu, gd = place_results(gh, gb, gu, gd)
    return (gh.T, gb, gu.T, gd)


def solution(mesh):
    placed = (
        P("group", "tensor"),
        P("tensor", "group"),
        P(None, "group"),
        P(None, "group"),
        P(),
        P(None, ("group", "tensor")),
        P(("group", "tensor"), None),
        P(),
    )
    return jax.shard_map(
        local,
        mesh=mesh,
        in_specs=placed,
        out_specs=(
            P("group", "tensor"),
            P("tensor", "group"),
            P(None, ("group", "tensor")),
            P(("group", "tensor"), None),
        ),
        check_vma=False,
    )
```

```python
import jax
import jax.numpy as jnp
from jax import lax
from jax.experimental import pallas as pl
from jax.experimental.pallas import tpu as pltpu
from jax.sharding import PartitionSpec as P

MESH = pl.DeviceIdType.MESH
F32 = jnp.float32
BF16 = jnp.bfloat16
GROUPS = 8
ZC = 8


def place():
    g = lax.axis_index("group")
    t = lax.axis_index("tensor")
    return g // 4, g % 4, t // 8, (t // 2) % 4, t % 2


def gid(xl, y):
    return xl * 4 + lax.rem(y, 4)


def tid(xh, z, c):
    return xh * 8 + lax.rem(z, 4) * 2 + c


class Copies:
    def __init__(self, send, recv):
        self.send, self.recv, self.made = send, recv, {}

    def start(self, k, src, dst, dev):
        cp = pltpu.make_async_remote_copy(
            src_ref=src, dst_ref=dst, send_sem=self.send.at[k], recv_sem=self.recv.at[k],
            device_id=dev, device_id_type=MESH,
        )
        cp.start()
        self.made[k] = cp

    def arrived(self, *ks):
        for k in ks:
            self.made[k].wait_recv()

    def finish(self):
        for cp in self.made.values():
            cp.wait_send()


def enter(peers):
    barrier = pltpu.get_barrier_semaphore()
    for dev in peers:
        pl.semaphore_signal(barrier, inc=1, device_id=dev, device_id_type=MESH)
    pl.semaphore_wait(barrier, len(peers))


OWN, ABOVE, BELOW, FAR = 0, 2, 4, 6


class PieceGather:
    def __init__(self, buf, cps, up, down, sib, at):
        self.buf, self.cps, self.up, self.down, self.sib, self.at = buf, cps, up, down, sib, at

    def begin(self, k):
        buf, at, n = self.buf, self.at[k], len(self.at)
        self.cps.start(k, buf.at[(OWN,) + at], buf.at[(BELOW,) + at], self.up)
        self.cps.start(n + k, buf.at[(OWN,) + at], buf.at[(ABOVE,) + at], self.down)

    def middle(self, k):
        buf, at, n = self.buf, self.at[k], len(self.at)
        self.cps.arrived(k, n + k)
        if k % 2 == 0:
            self.cps.start(2 * n + k, buf.at[(BELOW,) + at], buf.at[(FAR,) + at], self.up)
        else:
            self.cps.start(2 * n + k, buf.at[(ABOVE,) + at], buf.at[(FAR,) + at], self.down)

    def share(self, slot):
        self.cps.start(3 * len(self.at) + slot // 2, self.buf.at[slot], self.buf.at[slot + 1], self.sib)

    def shared(self, *slots):
        self.cps.arrived(*(3 * len(self.at) + slot // 2 for slot in slots))

    def last(self):
        n = len(self.at)
        self.cps.arrived(*range(2 * n, 3 * n))
        self.share(FAR)


NT = (((1,), (1,)), ((), ()))
TN = (((0,), (0,)), ((), ()))


def kernel(
    hidden_t, down_h, resid, grad, gain_h, w_up_t, w_down, places,
    gh_v, down, wu, wd,
    hid, gain, sel_of, rows, cots, normed,
    acc, sib_out, sib_in, z_out, z_in, x_out, x_in, pick_r, pick_c, resid_v, grad_v,
    pre, dact, act, dpre, act_t, dpre_t, v_out, v_in,
    stage, dn, sd_out, sd_in, far_out, far_in, dir_out, dir_in, sum_out, sum_in,
    drow, back_in, x2_out, x2_in, ds, fp, fin,
    a_s, a_r, ca_s, ca_r, cg_s, cg_r, sb_s, sb_r, z_s, z_r, x_s, x_r, ra_s, ra_r, rg_s, rg_r,
    sd_s, sd_r, fr_s, fr_r, nd_s, nd_r, ns_s, ns_r, ba_s, ba_r, x2_s, x2_r, dg_s, dg_r, f_s, f_r, v_s, v_r, local_sem,
):
    where = place()
    xl, y, xh, z, c = where
    g, t = gid(xl, y), tid(xh, z, c)
    me = z * 2 + c
    head = g // 2
    width = resid.shape[1]
    model = rows.shape[2]
    inner = hid.shape[1]
    slots = rows.shape[1]
    part = inner // 2
    quarter = inner // 4

    loads = [pltpu.make_async_copy(hidden_t, hid.at[g], local_sem.at[0])]
    for i in range(2):
        tok = pl.ds(pl.multiple_of((8 * i + me) * 64, 64), 64)
        loads.append(pltpu.make_async_copy(grad.at[tok], grad_v.at[pl.ds(64 * i, 64)], local_sem.at[1 + i]))
        loads.append(pltpu.make_async_copy(resid.at[tok], resid_v.at[pl.ds(64 * i, 64)], local_sem.at[3 + i]))
    loads.append(pltpu.make_async_copy(places, sel_of, local_sem.at[8]))
    loads.append(pltpu.make_async_copy(gain_h, gain, local_sem.at[9]))
    late = [
        pltpu.make_async_copy(down_h, down, local_sem.at[5]),
        pltpu.make_async_copy(w_down, wd, local_sem.at[6]),
        pltpu.make_async_copy(w_up_t, wu, local_sem.at[7]),
    ]
    for cp in loads + late[:1]:
        cp.start()

    xp = (gid(1 - xl, y), t)
    yp, ym = (gid(xl, y + 1), t), (gid(xl, y + 3), t)
    sib = (g, tid(xh, z, 1 - c))
    xhp = (g, tid(1 - xh, z, c))
    zup, zdown = (g, tid(xh, z + 1, c)), (g, tid(xh, z + 3, c))
    group_peers = [(lax.rem(g + k, GROUPS), t) for k in range(1, GROUPS)]
    z_peers = [(g, tid(xh, z + k, c)) for k in range(1, 4)]
    cross_peers = [(g, tid(xh, z + k, 1 - c)) for k in range(1, 4)]
    with jax.named_scope("enter"):
        enter(group_peers + z_peers + cross_peers + [sib, xhp])
        for cp in loads:
            cp.wait()

    a, ca, cg, sb = Copies(a_s, a_r), Copies(ca_s, ca_r), Copies(cg_s, cg_r), Copies(sb_s, sb_r)
    xx, ra, rg = Copies(x_s, x_r), Copies(ra_s, ra_r), Copies(rg_s, rg_r)
    sd, fr, nd, ns = Copies(sd_s, sd_r), Copies(fr_s, fr_r), Copies(nd_s, nd_r), Copies(ns_s, ns_r)
    ba, x2, dg, f = Copies(ba_s, ba_r), Copies(x2_s, x2_r), Copies(dg_s, dg_r), Copies(f_s, f_r)
    vx = Copies(v_s, v_r)

    low, high = pl.ds(0, part), pl.ds(part, part)
    by_x = inner // 6 // 16 * 16
    low_x, low_y = pl.ds(0, by_x), pl.ds(by_x, part - by_x)
    high_x, high_y = pl.ds(part, by_x), pl.ds(part + by_x, part - by_x)

    def pass_hidden(k, shard, rows_of, to):
        piece = hid.at[shard, rows_of]
        a.start(k, piece, piece, to)

    def cols(j):
        return pl.ds(pl.multiple_of(j * width, 128), width)

    def select():
        lane = lax.broadcasted_iota(jnp.int32, (128, 4 * slots), 1)
        token = lax.broadcasted_iota(jnp.int32, (128, 4 * slots), 0)
        second = lax.rem(lane, slots) >= slots // 2
        places = [sel_of[8 * i + me, h : h + 1, :] for h in range(4) for i in range(2)]
        wanted = jnp.broadcast_to(jnp.concatenate(places, axis=1), lane.shape)
        hit = (wanted >= 0) & (wanted + jnp.where(second, 64, 0) == token)
        return jnp.where(hit, 1.0, 0.0).astype(BF16)

    def deal(copies, picked, buf, values):
        chosen = lax.dot_general(select(), values, TN, preferred_element_type=F32)
        picked[...] = chosen.astype(BF16).reshape(picked.shape)
        for k in range(1, GROUPS):
            to = lax.rem(g + k, GROUPS)
            copies.start(k - 1, picked.at[to // 2], buf.at[OWN, :, cols(g)], (to, t))
        buf[OWN, :, cols(g)] = picked[head]

    deal(ca, pick_c, cots, grad_v[...])

    for k, rows_of, to in ((0, low, xp), (2, low, yp), (5, high, ym), (1, high, xp), (3, high, yp), (4, low, ym)):
        pass_hidden(k, g, rows_of, to)
    for cp in late[1:]:
        cp.start()

    columns = [(slice(None), cols(lax.rem(g + GROUPS - k, GROUPS))) for k in range(GROUPS)]
    cot_ring = PieceGather(cots, cg, zup, zdown, sib, columns)
    row_ring = PieceGather(rows, rg, zup, zdown, sib, columns)
    ds_ring = PieceGather(ds, dg, zup, zdown, sib, [(pl.ds(0, 64),), (pl.ds(64, 64),)])

    order = [
        (xl, y), (1 - xl, y), (xl, lax.rem(y + 3, 4)), (xl, lax.rem(y + 1, 4)), (xl, lax.rem(y + 2, 4)),
        (1 - xl, lax.rem(y + 3, 4)), (1 - xl, lax.rem(y + 1, 4)), (1 - xl, lax.rem(y + 2, 4)),
    ]

    def multiply(k):
        sx, sy = order[k]
        acc[k] = lax.dot_general(hid[gid(sx, sy)], down[...], TN, preferred_element_type=F32).reshape(2, 64, width)
        sib_out[k] = acc[k, 1 - c].astype(BF16)
        sb.start(k, sib_out.at[k], sib_in.at[k], sib)

    def z_copy(k):
        sx, sy = order[k]
        return pltpu.make_async_remote_copy(
            src_ref=z_out.at[k], dst_ref=z_in.at[sx, z], send_sem=z_s.at[k], recv_sem=z_r.at[sx, z],
            device_id=(g, tid(xh, sy, c)), device_id_type=MESH,
        )

    def pass_on(k):
        sx, sy = order[k]
        sb.arrived(k)
        z_out[k] = (acc[k, c] + sib_in[k].astype(F32)).astype(BF16)

        @pl.when(sy != z)
        def _():
            z_copy(k).start()

        @pl.when(sy == z)
        def _():
            z_in[sx, z] = z_out[k]

    k_step = 1024

    def product(total, values, weights, lo, hi):
        r = pl.ds(lo * slots, (hi - lo) * slots)
        total[r, :] = jnp.zeros(((hi - lo) * slots, total.shape[1]), F32)

        @pl.loop(0, model // k_step)
        def _(k):
            kc = pl.ds(pl.multiple_of(k * k_step, 128), k_step)
            total[r, :] += lax.dot_general(
                values[lo:hi, :, kc].reshape((hi - lo) * slots, k_step), weights[:, kc], NT,
                preferred_element_type=F32,
            )

    with jax.named_scope("gather_hidden"):
        late[0].wait()
        multiply(0)
        before, after, beside, far = gid(xl, y + 3), gid(xl, y + 1), gid(1 - xl, y), gid(xl, y + 2)
        cot_ring.begin(0)
        for k in range(1, GROUPS):
            ca.arrived(k - 1)
            cot_ring.begin(k)
        cot_ring.share(OWN)
        a.arrived(2)
        pass_hidden(6, before, low, yp)
        a.arrived(5)
        pass_hidden(7, after, high, ym)
        a.arrived(0)
        pass_hidden(14, before, low_x, xp)
        pass_hidden(15, after, high_x, xp)
        pass_hidden(8, beside, low_y, yp)
        pass_hidden(10, beside, low, ym)
        a.arrived(1)
        pass_hidden(9, beside, high, yp)
        pass_hidden(11, beside, high_y, ym)
        multiply(1)
        pass_on(0)
        a.arrived(3)
        multiply(2)
        pass_on(1)
        a.arrived(4)
        multiply(3)
        pass_on(2)
        a.arrived(6)
        pass_hidden(12, far, low, xp)
        a.arrived(7)
        pass_hidden(13, far, high, xp)
        multiply(4)
        pass_on(3)
        pass_on(4)
    with jax.named_scope("gather_cots"):
        for k in range(GROUPS):
            cot_ring.middle(k)
        cot_ring.share(BELOW)
        cot_ring.share(ABOVE)
    with jax.named_scope("gather_rest"):
        a.arrived(8, 9, 14)
        multiply(5)
        a.arrived(10, 11, 15)
        multiply(6)
        pass_on(5)
        pass_on(6)
        a.arrived(12, 13)
        multiply(7)
        pass_on(7)
    with jax.named_scope("sum_stream"):
        for i, sx in enumerate((xl, 1 - xl)):
            for dz in range(1, 4):
                src = lax.rem(z + dz, 4)
                pltpu.make_async_remote_copy(
                    src_ref=z_out.at[0], dst_ref=z_in.at[sx, src], send_sem=z_s.at[0], recv_sem=z_r.at[sx, src],
                    device_id=(g, tid(xh, z + dz, c)), device_id_type=MESH,
                ).wait_recv()
            parts = z_in[sx].astype(F32)
            x_out[sx] = ((parts[0] + parts[1]) + (parts[2] + parts[3])).astype(BF16)
            xx.start(i, x_out.at[sx], x_in.at[sx], xhp)
        xx.arrived(0, 1)
        total = (x_out[...].astype(F32) + x_in[...].astype(F32)).reshape(2 * 64, width)
        stream = (resid_v[...].astype(F32) + total).astype(BF16)
    with jax.named_scope("deal_rows"):
        deal(ra, pick_r, rows, stream)
        row_ring.begin(0)
        cot_ring.last()
        for k in range(1, GROUPS):
            ra.arrived(k - 1)
            row_ring.begin(k)
        row_ring.share(OWN)

    def gain_at(j):
        return gain[pl.ds(head, 1), cols(j)]

    def norm_shard(slot):
        def add(j, squares):
            v = rows[slot, :, cols(j)].astype(F32)
            return squares + v * v

        squares = lax.fori_loop(0, GROUPS, add, jnp.zeros((slots, width), F32))
        inv = lax.rsqrt(jnp.sum(squares, axis=-1, keepdims=True) * (1.0 / model) + 1e-06)

        @pl.loop(0, GROUPS)
        def _(j):
            v = rows[slot, :, cols(j)].astype(F32)
            normed[slot, :, cols(j)] = (v * inv * gain_at(j)).astype(BF16)

        return inv

    def activate(slot):
        r = pl.ds(slot * slots, slots)
        p = pre[r, :]
        s = jax.nn.sigmoid(p)
        act[r, :] = (p * s).astype(BF16)
        d = (dact[r, :] * s * (1.0 + p * (1.0 - s))).astype(BF16)
        dpre[r, :] = d
        v_out[slot] = jnp.broadcast_to(jnp.sum(d.astype(F32) * p, axis=-1, keepdims=True), v_out.shape[1:])

    with jax.named_scope("gather_rows"):
        cot_ring.shared(OWN, BELOW, ABOVE, FAR)
        late[1].wait()
        late[2].wait()
        inv_own = norm_shard(OWN)
        product(dact, cots, wd, 0, 8)
        for k in range(GROUPS):
            row_ring.middle(k)
        row_ring.share(BELOW)
        row_ring.share(ABOVE)
        row_ring.shared(OWN)
        norm_shard(OWN + 1)
        norm_shard(BELOW)
        norm_shard(ABOVE)
        row_ring.shared(BELOW)
        row_ring.shared(ABOVE)
        norm_shard(BELOW + 1)
        norm_shard(ABOVE + 1)
        row_ring.last()
        product(pre, normed, wu, 0, FAR)
        for slot in range(FAR):
            activate(slot)
        norm_shard(FAR)
        row_ring.shared(FAR)
        norm_shard(FAR + 1)

    with jax.named_scope("heads"):
        product(pre, normed, wu, FAR, 8)
        activate(FAR)
        activate(FAR + 1)
        for slot in range(1, 8):
            core = 1 - c if slot % 2 else c
            vx.start(slot - 1, v_out.at[slot], v_in.at[slot], (g, tid(xh, z + (0, 1, 3, 2)[slot // 2], core)))

    def dn_multiply(i):
        stage[...] = jnp.dot(
            dpre[...], wu[:, cols(lax.rem(g + i, GROUPS))], preferred_element_type=F32
        ).reshape(stage.shape)
        dn[i] = stage[:, 0]
        sd_out[i] = stage[:, 1].astype(BF16)
        sd.start(i, sd_out.at[i], sd_in.at[i], sib)

    def toward(i):
        return (zup, zdown, ABOVE // 2, BELOW // 2) if i % 2 == 0 else (zdown, zup, BELOW // 2, ABOVE // 2)

    def dn_split(i):
        to, other, z_to, z_other = toward(i)
        sd.arrived(i)
        dn[i] = dn[i] + sd_in[i].astype(F32)
        far_out[i] = dn[i, FAR // 2].astype(BF16)
        fr.start(i, far_out.at[i], far_in.at[i], to)
        dir_out[i] = dn[i, z_other].astype(BF16)
        nd.start(i, dir_out.at[i], dir_in.at[i], other)

    def dn_forward(i):
        to, other, z_to, z_other = toward(i)
        fr.arrived(i)
        sum_out[i] = (dn[i, z_to] + far_in[i].astype(F32)).astype(BF16)
        ns.start(i, sum_out.at[i], sum_in.at[i], to)

    def dn_finish(i):
        to = lax.rem(g + i, GROUPS)
        ns.arrived(i)
        nd.arrived(i)
        q = (dn[i, 0] + sum_in[i].astype(F32) + dir_in[i].astype(F32)) * gain_at(to)
        value = (inv_own * q - rows[OWN, :, cols(to)].astype(F32) * back).astype(BF16)
        if i == 0:
            back_in[lax.rem(g, 2), head] = value
        else:
            drow[i] = value
            ba.start(i - 1, drow.at[i], back_in.at[lax.rem(g, 2), head], (to, t))

    with jax.named_scope("row_gradients"):
        for i in range(GROUPS + 3):
            if i < 8:
                dn_multiply(i)
            if 0 <= i - 1 < 8:
                dn_split(i - 1)
            if 0 <= i - 3 < 8:
                dn_forward(i - 3)
        vx.arrived(*range(7))
        v = v_out[0]
        for slot in range(1, 8):
            v = v + v_in[slot]
        back = inv_own * inv_own * (v[:, :1] * (1.0 / model))

    def down_grad(j):
        wd[:, cols(j)] = jnp.dot(
            act_t[...], cots[:, :, cols(j)].reshape(ZC * slots, width), preferred_element_type=F32
        ).astype(BF16)

    def up_grad(j):
        wu[:, cols(j)] = jnp.dot(
            dpre_t[...], normed[:, :, cols(j)].reshape(ZC * slots, width), preferred_element_type=F32
        ).astype(BF16)

    with jax.named_scope("down_grads"):
        act_t[...] = act[...].T
        dpre_t[...] = dpre[...].T
    with jax.named_scope("norm_backward"):
        for i in range(GROUPS):
            dn_finish(i)

    with jax.named_scope("return_rows"):
        pl.loop(0, 4)(down_grad)
        ba.arrived(*range(GROUPS - 1))
        chosen = select()
        x2_out[...] = (
            jnp.dot(chosen, back_in[0].reshape(4 * slots, width), preferred_element_type=F32)
            + jnp.dot(chosen, back_in[1].reshape(4 * slots, width), preferred_element_type=F32)
        ).astype(BF16)
        halves = (pl.ds(0, 64), pl.ds(64, 64))
        for i, h in enumerate(halves):
            x2.start(i, x2_out.at[h], x2_in.at[h], xhp)
        pl.loop(4, GROUPS)(down_grad)
        pl.loop(0, 3)(up_grad)
        for i, h in enumerate(halves):
            x2.arrived(i)
            ds[OWN, h, :] = (
                grad_v[h, :].astype(F32) + (x2_out[h, :].astype(F32) + x2_in[h, :].astype(F32))
            ).astype(BF16)
            ds_ring.begin(i)
        ds_ring.share(OWN)
    with jax.named_scope("gather_dstream"):
        pl.loop(3, 6)(up_grad)
        ds_ring.middle(0)
        ds_ring.middle(1)
        ds_ring.share(BELOW)
        ds_ring.share(ABOVE)
        ds_ring.last()
        ds_ring.shared(OWN, BELOW, ABOVE, FAR)

    def tokens_of(sx, sy):
        ahead = lax.rem(sy + 4 - z, 4)
        slot = jnp.where(ahead == 3, BELOW, jnp.where(ahead == 2, FAR, ahead * 2))
        at = pl.ds(pl.multiple_of(sx * 64, 64), 64)
        return [ds[slot + c, at, :], ds[slot + 1 - c, at, :]]

    def hidden_grads(i, first, second, r):
        both = jnp.concatenate(tokens_of(*first) + tokens_of(*second), axis=0)
        p = lax.dot_general(down[r, :], both, NT, preferred_element_type=F32).astype(BF16)
        fp[i, r, :] = p[:, :128]
        fp[i + 1, r, :] = p[:, 128:]

    y1, y2, y3 = lax.rem(y + 1, 4), lax.rem(y + 2, 4), lax.rem(y + 3, 4)
    quarters = [pl.ds(m * quarter, quarter) for m in range(4)]

    def f_start(kind, m, src, dst, to):
        r = quarters[m]
        f.start(kind * 4 + m, fp.at[src, r], fin.at[dst, r], to)

    def f_sum(dst, m, *terms):
        r = quarters[m]
        total = fp[dst, r, :].astype(F32)
        for term in terms:
            total = total + fin[term, r, :].astype(F32)
        return total.astype(BF16)

    def f_begin(m):
        r = quarters[m]
        hidden_grads(2, (1 - xl, y1), (1 - xl, y3), r)
        f_start(0, m, 2, 0, yp)
        f_start(1, m, 3, 1, ym)
        hidden_grads(0, (1 - xl, y2), (xl, y2), r)
        f_start(2, m, 0, 2, xp)
        hidden_grads(4, (xl, y1), (xl, y3), r)
        hidden_grads(6, (1 - xl, y), (xl, y), r)

    def f_far(m):
        f.arrived(8 + m)
        fp[1, quarters[m], :] = f_sum(1, m, 2)
        f_start(4, m, 1, 6, yp if m % 2 == 0 else ym)

    def f_direct(m):
        if m % 2 == 0:
            f_start(3, m, 5, 4, ym)
        else:
            f_start(3, m, 4, 3, yp)

    def f_side(m):
        f.arrived(m, 4 + m)
        fp[6, quarters[m], :] = f_sum(6, m, 0, 1)
        f_start(5, m, 6, 5, xp)

    def f_near(m):
        f.arrived(16 + m)
        i = 4 if m % 2 == 0 else 5
        fp[i, quarters[m], :] = f_sum(i, m, 6)
        f_start(6, m, i, i - 1, yp if m % 2 == 0 else ym)

    def f_end(m):
        f.arrived(12 + m, 20 + m, 24 + m)
        gh_v[quarters[m], :] = f_sum(7, m, 3, 4, 5)

    def backbone_grad(m):
        r = pl.ds(pl.multiple_of(m * quarter, 16), quarter)
        total = jnp.zeros((quarter, width), F32)
        for i in range(4):
            left = jnp.concatenate([hid[2 * i, r, :], hid[2 * i + 1, r, :]], axis=1)
            right = jnp.concatenate(
                tokens_of((2 * i) // 4, (2 * i) % 4) + tokens_of((2 * i + 1) // 4, (2 * i + 1) % 4), axis=0)
            total = total + jnp.dot(left, right, preferred_element_type=F32)
        down[r, :] = total.astype(BF16)

    with jax.named_scope("hidden_grads"):
        for m in range(4):
            f_begin(m)
    with jax.named_scope("sum_hidden_grads"):
        for m in range(4):
            f_far(m)
        for m in range(4):
            f_direct(m)
        f_side(0)
        pl.loop(6, 8)(up_grad)
        pl.loop(0, 2)(backbone_grad)
        f_side(1)
        f_near(0)
        f_near(1)
        f_side(2)
        f_side(3)
        pl.loop(2, 4)(backbone_grad)
        f_near(2)
        f_near(3)
        for m in range(4):
            f_end(m)

    with jax.named_scope("finish"):
        for cps in (a, ca, cg, sb, xx, ra, rg, sd, fr, nd, ns, ba, x2, dg, f, vx):
            cps.finish()
        for k in range(GROUPS):
            @pl.when(order[k][1] != z)
            def _():
                z_copy(k).wait_send()


def run(hidden_t, down, resid, grad, gain, w_up_t, w_down, places):
    inner, tokens = hidden_t.shape
    width = down.shape[1]
    slots = 2 * places.shape[2]
    model = width * GROUPS
    units = w_down.shape[0]
    any_spec = pl.BlockSpec(memory_space=pl.ANY)
    vmem = pl.BlockSpec(memory_space=pltpu.VMEM)
    dma = pltpu.SemaphoreType.DMA
    sems = []
    for n in ((16,), (7,), (28,), (8,)):
        sems += [dma(n), dma(n)]
    sems += [dma((8,)), dma((2, 4))]
    for n in ((2,), (7,), (28,), (8,), (8,), (8,), (8,), (7,), (2,), (10,), (28,), (7,)):
        sems += [dma(n), dma(n)]
    sems += [dma((10,))]
    piece = (64, width)
    return pl.pallas_call(
        kernel,
        out_shape=(
            pltpu.VMEM((inner, tokens), BF16),
            pltpu.VMEM((inner, width), BF16),
            pltpu.VMEM((units, model), BF16),
            pltpu.VMEM((units, model), BF16),
        ),
        in_specs=[any_spec] * 8,
        out_specs=(vmem,) * 4,
        scratch_shapes=[
            pltpu.VMEM((GROUPS, inner, tokens), BF16),
            pltpu.VMEM((4, model), F32),
            pltpu.VMEM(places.shape, jnp.int32),
            pltpu.VMEM((ZC, slots, model), BF16),
            pltpu.VMEM((ZC, slots, model), BF16),
            pltpu.VMEM((ZC, slots, model), BF16),
            pltpu.VMEM((8, 2) + piece, F32),
            pltpu.VMEM((8,) + piece, BF16),
            pltpu.VMEM((8,) + piece, BF16),
            pltpu.VMEM((8,) + piece, BF16),
            pltpu.VMEM((2, 4) + piece, BF16),
            pltpu.VMEM((2,) + piece, BF16),
            pltpu.VMEM((2,) + piece, BF16),
            pltpu.VMEM((4, slots, width), BF16),
            pltpu.VMEM((4, slots, width), BF16),
            pltpu.VMEM((128, width), BF16),
            pltpu.VMEM((128, width), BF16),
            pltpu.VMEM((ZC * slots, units), F32),
            pltpu.VMEM((ZC * slots, units), F32),
            pltpu.VMEM((ZC * slots, units), BF16),
            pltpu.VMEM((ZC * slots, units), BF16),
            pltpu.VMEM((units, ZC * slots), BF16),
            pltpu.VMEM((units, ZC * slots), BF16),
            pltpu.VMEM((ZC, slots, 128), F32),
            pltpu.VMEM((ZC, slots, 128), F32),
            pltpu.VMEM((4, 2, slots, width), F32),
            pltpu.VMEM((8, 4, slots, width), F32),
            pltpu.VMEM((8, 4, slots, width), BF16),
            pltpu.VMEM((8, 4, slots, width), BF16),
        ]
        + [pltpu.VMEM((8, slots, width), BF16)] * 6
        + [
            pltpu.VMEM((8, slots, width), BF16),
            pltpu.VMEM((2, 4, slots, width), BF16),
            pltpu.VMEM((128, width), BF16),
            pltpu.VMEM((128, width), BF16),
            pltpu.VMEM((8, 128, width), BF16),
            pltpu.VMEM((8, inner, tokens), BF16),
            pltpu.VMEM((7, inner, tokens), BF16),
        ]
        + sems,
        compiler_params=pltpu.CompilerParams(
            collective_id=0, has_side_effects=True, vmem_limit_bytes=50 * 1024 * 1024
        ),
        name="backbone_and_heads",
    )(hidden_t, down, resid, grad, gain, w_up_t, w_down, places)


def copy_kernel(*refs):
    n = (len(refs) - 1) // 2
    copies = []
    for src, dst in zip(refs[:n], refs[n : 2 * n]):
        step = src.shape[0] // 3
        for r in range(0, src.shape[0], step):
            rows_of = pl.ds(r, step)
            copies.append(pltpu.make_async_copy(src.at[rows_of], dst.at[rows_of], refs[-1].at[len(copies)]))
    for cp in copies:
        cp.start()
    for cp in copies:
        cp.wait()


def place_results(*arrays):
    return pl.pallas_call(
        copy_kernel,
        out_shape=tuple(jax.ShapeDtypeStruct(a.shape, a.dtype) for a in arrays),
        in_specs=[pl.BlockSpec(memory_space=pltpu.VMEM)] * len(arrays),
        out_specs=(pl.BlockSpec(memory_space=pl.ANY),) * len(arrays),
        scratch_shapes=[pltpu.SemaphoreType.DMA((3 * len(arrays),))],
        compiler_params=pltpu.CompilerParams(vmem_limit_bytes=4 * 1024 * 1024),
        name="place_results",
    )(*arrays)


def local(backbone_hidden, backbone_down, residual, head_grad, gain, w_up, w_down, route):
    gh, gb, gu, gd = run(
        backbone_hidden.T, backbone_down, residual, head_grad, gain, w_up.T, w_down, route
    )
    gh, gb, gu, gd = place_results(gh, gb, gu, gd)
    return (gh.T, gb, gu.T, gd)


def solution(mesh):
    placed = (
        P("group", "tensor"),
        P("tensor", "group"),
        P(None, "group"),
        P(None, "group"),
        P(),
        P(None, ("group", "tensor")),
        P(("group", "tensor"), None),
        P(),
    )
    return jax.shard_map(
        local,
        mesh=mesh,
        in_specs=placed,
        out_specs=(
            P("group", "tensor"),
            P("tensor", "group"),
            P(None, ("group", "tensor")),
            P(("group", "tensor"), None),
        ),
        check_vma=False,
    )
```
